256 devices in a mesh: fluid: 64 (over x, z, core), metal: 4 (over y).
Axes of the slice: x: 4, y: 4, z: 8, core: 2. Of those that a mesh axis runs over, the one named last changes fastest.
Arguments:
- fluid_x: bfloat16 [16384, 512], P('fluid', 'metal'), may hold values from -32 to 32
- metal_x: bfloat16 [8192, 512], P('fluid', 'metal'), may hold values from -32 to 32
- w_rf: bfloat16 [512, 512], P(None, 'metal'), may hold values from -0.5 to 0.5
- w_vf: bfloat16 [512, 512], P(None, 'metal'), may hold values from -0.25 to 0.25
- w_rm: bfloat16 [512, 512], P(None, 'metal'), may hold values from -0.5 to 0.5
- w_vm: bfloat16 [512, 512], P(None, 'metal'), may hold values from -0.25 to 0.25
- fluid_grad: bfloat16 [16384, 512], P('fluid', 'metal'), may hold values from -6 to 6
- metal_grad: bfloat16 [8192, 512], P('fluid', 'metal'), may hold values from -6 to 6
- pair_list: int32 [2048, 2], P('fluid'), may hold values from 0 to 63, as said below
- pair_count: int32 [64], P('fluid'), may hold values from 2 to 32, as said below
Outputs:
- fluid_out: bfloat16 [16384, 512], P('fluid', 'metal')
- metal_out: bfloat16 [8192, 512], P('fluid', 'metal')
- fluid_dx: bfloat16 [16384, 512], P('fluid', 'metal')
- metal_dx: bfloat16 [8192, 512], P('fluid', 'metal')
- weight_grads: float32 [4, 512, 512], P(None, None, 'metal')
The draws below stay inside these ranges and needn't reach their ends.
Inputs may be any that keep to these rules, and one draw needn't show every extreme that they name: `pair_list`: column 0 is a local fluid block below 2, column 1 a metal block below 64. The first pair_count[d] entries of fluid index d are distinct pairs; every fluid block of every index and every metal block stands in some live entry; entries past the count hold valid indices and are ignored. `pair_count`: some fluid index has all 32 slots live.
All inputs are finite; a program needn't handle non-finite values.
Results may differ from the reference program's by a relative error of at most 0.0179.
The reference program's roundings to bfloat16 on the way (of `scaled_grad`) count: a program that leaves them out, or rounds other values in their place, can miss the bound.
Values may be sent and summed in bfloat16 or wider, within the bound.
No kernel may reach another device: no remote copies, remote signals or barrier semaphores. Data moves between devices by JAX's collectives and lax.ppermute only.
A program may use at most 128 MiB of HBM per device.

```python
import math
import jax
import jax.numpy as jnp
from jax import lax

D = 512
H = 8
DH = 64
BLK = 128
FT = 256
FBD = 2
PAIRS = 32
NF = 16384
NM = 8192
N_FLUID = 64


def token_block(key, rows, shift):
    key = jax.random.fold_in(key, 11 + shift)
    layout = jax.random.truncated_normal(key, -6.0, 6.0, (N_FLUID, rows, D), jnp.float32)
    return layout.reshape(N_FLUID * rows, D).astype(jnp.bfloat16)


def draw_fluid_x(key, part):
    return token_block(key, FT, 0)


def draw_metal_x(key, part):
    return token_block(key, BLK, 1)


def projection(key, shift):
    key = jax.random.fold_in(key, 21 + shift)
    own_part = jax.random.normal(key, (D, D), jnp.float32) / math.sqrt(D)
    values = own_part
    return jnp.clip(values, -0.4, 0.4).astype(jnp.bfloat16)


def draw_w_rf(key, part):
    return projection(key, 0)


def draw_w_rm(key, part):
    return projection(key, 1)


def pair_tables(key):
    key = jax.random.fold_in(key, 202)
    count_key, full_key, rank_key = jax.random.split(key, 3)
    counts = jax.random.randint(count_key, (N_FLUID,), FBD, PAIRS + 1, dtype=jnp.int32)
    fullest = jax.random.randint(full_key, (), 0, N_FLUID, dtype=jnp.int32)
    counts = jnp.where(jnp.arange(N_FLUID, dtype=jnp.int32) == fullest, PAIRS, counts).astype(jnp.int32)
    cell_total = FBD * N_FLUID

    def shuffled(subkey):
        return jax.random.permutation(subkey, cell_total).astype(jnp.int32)
    priority = jax.vmap(shuffled)(jax.random.split(rank_key, N_FLUID))
    device = jnp.arange(N_FLUID, dtype=jnp.int32)[:, None]
    cell_index = jnp.arange(cell_total, dtype=jnp.int32)[None, :]
    fluid_part = cell_index // N_FLUID
    metal_part = cell_index % N_FLUID
    needed = metal_part == (device + fluid_part) % N_FLUID
    priority = jnp.where(needed, priority, priority + cell_total)
    chosen = jnp.argsort(priority, axis=1, stable=True)[:, :PAIRS].astype(jnp.int32)
    pair_table = jnp.stack([chosen // N_FLUID, chosen % N_FLUID], axis=-1).reshape(N_FLUID * PAIRS, 2)
    return (pair_table.astype(jnp.int32), counts)


def draw_pair_list(key, part):
    return pair_tables(key)[0]


def draw_pair_count(key, part):
    return pair_tables(key)[1]


def shard_levels(own_key, extent, cuts, least, high):
    def one(dim, blocks):
        steps = jax.random.uniform(jax.random.fold_in(jax.random.fold_in(own_key, 6), dim), (blocks,), jnp.float32, least / len(cuts), high / len(cuts))
        return jnp.repeat(jnp.exp(steps), extent[dim] // blocks).reshape((-1,) + (1,) * (len(extent) - dim - 1))

    level = one(*cuts[0])
    for cut in cuts[1:]:
        level = level * one(*cut)
    return level


def centred(own_key, shape, deviation, reach, shards=(), kind=jnp.bfloat16):
    factor_of = shard_levels(own_key, shape, shards, -0.22, 0.18) if shards else 1.0
    drawn = jax.random.normal(own_key, shape, jnp.float32) * deviation * factor_of
    return jnp.minimum(jnp.maximum(drawn, -reach), reach).astype(kind)


def setup_inputs(seed: int = 0) -> dict:
    arg_keys = jax.random.split(jax.random.key(seed), 11)
    return {
        "fluid_x": draw_fluid_x(jax.random.fold_in(arg_keys[10], 71), 0),
        "metal_x": draw_metal_x(jax.random.fold_in(arg_keys[10], 71), 0),
        "w_rf": draw_w_rf(jax.random.fold_in(arg_keys[10], 71), 0),
        "w_vf": centred(arg_keys[3], (D, D), D ** -0.5, 0.25, ((1, 4),)),
        "w_rm": draw_w_rm(jax.random.fold_in(arg_keys[10], 71), 0),
        "w_vm": centred(arg_keys[5], (D, D), D ** -0.5, 0.25, ((1, 4),)),
        "fluid_grad": centred(arg_keys[6], (NF, D), 1.0, 6.0, ((0, 64), (1, 4))),
        "metal_grad": centred(arg_keys[7], (NM, D), 1.0, 6.0, ((0, 64), (1, 4))),
        "pair_list": draw_pair_list(jax.random.fold_in(arg_keys[10], 71), 0),
        "pair_count": draw_pair_count(jax.random.fold_in(arg_keys[10], 71), 0),
    }


LOWEST = -1e+30

def project(inputs, weight):
    return jnp.dot(inputs, weight, preferred_element_type=jnp.float32).astype(jnp.bfloat16)

def to_wide(values):
    return values.astype(jnp.float32)

def narrow(values):
    return lax.optimization_barrier(values.astype(jnp.bfloat16)).astype(jnp.float32)

def reference(fluid_x, metal_x, w_rf, w_vf, w_rm, w_vm, fluid_grad, metal_grad, pair_list, pair_count):
    inv_root = 1.0 / math.sqrt(DH)
    fluid_keys = project(fluid_x, w_rf)
    fluid_values = project(fluid_x, w_vf)
    metal_keys = project(metal_x, w_rm)
    metal_values = project(metal_x, w_vm)
    fluid_blocks = NF // BLK
    fkey_tiles = fluid_keys.reshape(fluid_blocks, BLK, H, DH)
    fval_tiles = fluid_values.reshape(fluid_blocks, BLK, H, DH)
    mkey_tiles = metal_keys.reshape(N_FLUID, BLK, H, DH)
    mval_tiles = metal_values.reshape(N_FLUID, BLK, H, DH)
    pair_total = N_FLUID * PAIRS
    batch_size = math.gcd(PAIRS, 16)
    batch_count = pair_total // batch_size
    slot_index = jnp.arange(pair_total, dtype=jnp.int32)
    owner_index = slot_index // PAIRS
    live_mask = slot_index % PAIRS < pair_count[owner_index]
    fblock = (owner_index * FBD + pair_list[:, 0]).astype(jnp.int32)
    mblock = pair_list[:, 1].astype(jnp.int32)
    batches = (fblock.reshape(batch_count, batch_size), mblock.reshape(batch_count, batch_size), live_mask.reshape(batch_count, batch_size))

    def scores_of(frows, mrows):
        return jnp.einsum('pahd,pbhd->phab', to_wide(fkey_tiles[frows]), to_wide(mkey_tiles[mrows])) * inv_root

    def max_pass(state, batch):
        row_max, col_max = state
        frows, mrows, active = batch
        scores = scores_of(frows, mrows)
        live = active[:, None, None]
        row_max = row_max.at[frows].max(jnp.where(live, lax.optimization_barrier(jnp.max(scores, axis=3)), LOWEST))
        col_max = col_max.at[mrows].max(jnp.where(live, lax.optimization_barrier(jnp.max(scores, axis=2)), LOWEST))
        return ((row_max, col_max), None)
    start_state = (jnp.full((fluid_blocks, H, BLK), LOWEST, jnp.float32), jnp.full((N_FLUID, H, BLK), LOWEST, jnp.float32))
    (row_max, col_max), _ = lax.scan(max_pass, start_state, batches)

    def sum_pass(state, batch):
        row_sum, fluid_num, col_sum, metal_num = state
        frows, mrows, active = batch
        scores = scores_of(frows, mrows)
        live = active[:, None, None, None]
        row_exp = jnp.where(live, jnp.exp(scores - row_max[frows][:, :, :, None]), 0.0)
        col_exp = jnp.where(live, jnp.exp(scores - col_max[mrows][:, :, None, :]), 0.0)
        row_sum = row_sum.at[frows].add(lax.optimization_barrier(jnp.sum(row_exp, axis=3)))
        col_sum = col_sum.at[mrows].add(lax.optimization_barrier(jnp.sum(col_exp, axis=2)))
        fluid_num = fluid_num.at[frows].add(jnp.einsum('phab,pbhd->pahd', narrow(row_exp), to_wide(mval_tiles[mrows])))
        metal_num = metal_num.at[mrows].add(jnp.einsum('phab,pahd->pbhd', narrow(col_exp), to_wide(fval_tiles[frows])))
        return ((row_sum, fluid_num, col_sum, metal_num), None)
    start_state = (jnp.zeros((fluid_blocks, H, BLK), jnp.float32), jnp.zeros((fluid_blocks, BLK, H, DH), jnp.float32), jnp.zeros((N_FLUID, H, BLK), jnp.float32), jnp.zeros((N_FLUID, BLK, H, DH), jnp.float32))
    (row_sum, fluid_num, col_sum, metal_num), _ = lax.scan(sum_pass, start_state, batches)
    fluid_out = (fluid_num / row_sum.transpose(0, 2, 1)[:, :, :, None]).reshape(NF, D).astype(jnp.bfloat16)
    metal_out = (metal_num / col_sum.transpose(0, 2, 1)[:, :, :, None]).reshape(NM, D).astype(jnp.bfloat16)
    col_rows = col_sum.transpose(0, 2, 1).reshape(NM, H)
    scaled_grad = (to_wide(metal_grad).reshape(NM, H, DH) / col_rows[:, :, None]).reshape(NM, D).astype(jnp.bfloat16)
    delta_f = lax.optimization_barrier(jnp.sum((to_wide(fluid_grad) * to_wide(fluid_out)).reshape(NF, H, DH), axis=2))
    delta_m = lax.optimization_barrier(jnp.sum((to_wide(scaled_grad) * to_wide(metal_out)).reshape(NM, H, DH), axis=2))
    grad_tiles = fluid_grad.reshape(fluid_blocks, BLK, H, DH)
    scaled_tiles = scaled_grad.reshape(N_FLUID, BLK, H, DH)
    dfluid_tiles = delta_f.reshape(fluid_blocks, BLK, H)
    dmetal_tiles = delta_m.reshape(N_FLUID, BLK, H)

    def grad_pass(state, batch):
        grad_rf, grad_vf, grad_rm, grad_vm = state
        frows, mrows, active = batch
        scores = scores_of(frows, mrows)
        live = active[:, None, None, None]
        attn = jnp.where(live, jnp.exp(scores - row_max[frows][:, :, :, None]) / row_sum[frows][:, :, :, None], 0.0)
        col_exp = jnp.where(live, jnp.exp(scores - col_max[mrows][:, :, None, :]), 0.0)
        fluid_term = jnp.einsum('pahd,pbhd->phab', to_wide(grad_tiles[frows]), to_wide(mval_tiles[mrows]))
        metal_term = jnp.einsum('pahd,pbhd->phab', to_wide(fval_tiles[frows]), to_wide(scaled_tiles[mrows]))
        dscore = attn * (fluid_term - dfluid_tiles[frows].transpose(0, 2, 1)[:, :, :, None])
        dscore = dscore + col_exp * (metal_term - dmetal_tiles[mrows].transpose(0, 2, 1)[:, :, None, :])
        dscore_weight = narrow(dscore)
        grad_rf = grad_rf.at[frows].add(jnp.einsum('phab,pbhd->pahd', dscore_weight, to_wide(mkey_tiles[mrows])) * inv_root)
        grad_vf = grad_vf.at[frows].add(jnp.einsum('phab,pbhd->pahd', narrow(col_exp), to_wide(scaled_tiles[mrows])))
        grad_rm = grad_rm.at[mrows].add(jnp.einsum('phab,pahd->pbhd', dscore_weight, to_wide(fkey_tiles[frows])) * inv_root)
        grad_vm = grad_vm.at[mrows].add(jnp.einsum('phab,pahd->pbhd', narrow(attn), to_wide(grad_tiles[frows])))
        return ((grad_rf, grad_vf, grad_rm, grad_vm), None)
    start_state = (jnp.zeros((fluid_blocks, BLK, H, DH), jnp.float32), jnp.zeros((fluid_blocks, BLK, H, DH), jnp.float32), jnp.zeros((N_FLUID, BLK, H, DH), jnp.float32), jnp.zeros((N_FLUID, BLK, H, DH), jnp.float32))
    (grad_rf, grad_vf, grad_rm, grad_vm), _ = lax.scan(grad_pass, start_state, batches)
    grad_rf = grad_rf.reshape(NF, D).astype(jnp.bfloat16)
    grad_vf = grad_vf.reshape(NF, D).astype(jnp.bfloat16)
    grad_rm = grad_rm.reshape(NM, D).astype(jnp.bfloat16)
    grad_vm = grad_vm.reshape(NM, D).astype(jnp.bfloat16)
    fluid_dx = (jnp.dot(grad_rf, w_rf.T, preferred_element_type=jnp.float32) + jnp.dot(grad_vf, w_vf.T, preferred_element_type=jnp.float32)).astype(jnp.bfloat16)
    metal_dx = (jnp.dot(grad_rm, w_rm.T, preferred_element_type=jnp.float32) + jnp.dot(grad_vm, w_vm.T, preferred_element_type=jnp.float32)).astype(jnp.bfloat16)
    weight_grads = jnp.stack([jnp.dot(fluid_x.T, grad_rf, preferred_element_type=jnp.float32), jnp.dot(fluid_x.T, grad_vf, preferred_element_type=jnp.float32), jnp.dot(metal_x.T, grad_rm, preferred_element_type=jnp.float32), jnp.dot(metal_x.T, grad_vm, preferred_element_type=jnp.float32)])
    return (fluid_out, metal_out, fluid_dx, metal_dx, weight_grads)
```

```python
import functools

import jax
import jax.numpy as jnp
from jax import lax
from jax.experimental import pallas as pl
from jax.experimental.pallas import tpu as pltpu
from jax.sharding import Mesh, PartitionSpec as P

BLK = 128
HEADS = 2
DH = 64
NX, NZ, NC, NM = 4, 8, 2, 4
NG = NX * NC
FB = 2
NA = NG * FB
LOWEST = -1e30
ROOT = 0.125
XC = ("x", "c")
FLUID = ("x", "z", "c")
F_ROWS = 3 * FB * BLK + 16
M_ROWS = 3 * BLK
f32, bf16 = jnp.float32, jnp.bfloat16
PARAMS = pltpu.CompilerParams(vmem_limit_bytes=48 * 2**20)
VMEM = pl.BlockSpec(memory_space=pltpu.VMEM)
SMEM = pl.BlockSpec(memory_space=pltpu.SMEM)


def nn(a, b):
    return lax.dot_general(a, b, (((1,), (0,)), ((), ())), preferred_element_type=f32)


def nt(a, b):
    return lax.dot_general(a, b, (((1,), (1,)), ((), ())), preferred_element_type=f32)


def tn(a, b):
    return lax.dot_general(a, b, (((0,), (0,)), ((), ())), preferred_element_type=f32)


def head_mask(h):
    lane = lax.broadcasted_iota(jnp.int32, (BLK, BLK), 1)
    return lane < DH if h == 0 else lane >= DH


def of_head(tile, h):
    return jnp.where(head_mask(h), tile, jnp.zeros_like(tile))


def project_kernel(count, x, w_rf, w_vf, w_rm, w_vm, f_grad, m_grad, pairs, f_pay, m_pay):
    def project(rows, w):
        total = nn(x[0, rows], w[:BLK])
        for i in range(1, NM):
            total += nn(x[i, rows], w[i * BLK : (i + 1) * BLK])
        return total

    fluid, metal = slice(0, FB * BLK), slice(FB * BLK, FB * BLK + BLK)
    f_pay[0 : FB * BLK] = project(fluid, w_rf).astype(bf16)
    values = project(fluid, w_vf)
    for i in range(FB):
        start = (FB + i) * BLK
        f_pay[start : start + BLK] = values[i * BLK : (i + 1) * BLK].T.astype(bf16)
    f_pay[2 * FB * BLK : 3 * FB * BLK] = f_grad[...]
    slots = pairs.shape[0]
    code = pairs[:, 0:1] * (NX * NZ * NC) + pairs[:, 1:2]
    lane = lax.broadcasted_iota(jnp.int32, (slots, BLK), 1)
    slot = lax.broadcasted_iota(jnp.int32, (slots, BLK), 0)
    hit = jnp.where((code == lane) & (slot < count[0]), 1.0, 0.0)
    table = jnp.max(hit, axis=0, keepdims=True)
    f_pay[3 * FB * BLK :] = jnp.broadcast_to(table, (16, BLK)).astype(bf16)
    m_pay[0:BLK] = project(metal, w_rm).astype(bf16)
    m_pay[BLK : 2 * BLK] = project(metal, w_vm).astype(bf16)
    m_pay[2 * BLK :] = m_grad[...]


def f_tile(f_all, a, part):
    start = pl.multiple_of(part * FB * BLK + lax.rem(a, FB) * BLK, BLK)
    return f_all[lax.div(a, FB), pl.ds(start, BLK), :]


def forward_kernel(at, live, f_all, *refs):
    m_in = refs[:NZ]
    r_stat, c_stat, f_num, m_num, todo = refs[NZ : NZ + 5]
    m_key, m_valt, m_gradt = refs[NZ + 5 :]
    z = at[0]
    for s in range(NZ):
        j = lax.rem(z - s + NZ, NZ)
        m_key[j] = m_in[s][0:BLK]
        m_valt[j] = m_in[s][BLK : 2 * BLK].astype(f32).T.astype(bf16)
        m_gradt[j] = m_in[s][2 * BLK : 3 * BLK].astype(f32).T

    def list_step(i, n):
        todo[n] = i
        return n + live[i]

    total = lax.fori_loop(0, NA * NZ, list_step, 0)
    todo[NA * NZ] = total
    nr, nc = HEADS * NA, HEADS * NZ
    r_stat[0:nr] = jnp.full((nr, BLK), LOWEST, f32)
    r_stat[nr:] = jnp.zeros((2 * nr, BLK), f32)
    c_stat[0:nc] = jnp.full((nc, BLK), LOWEST, f32)
    c_stat[nc:] = jnp.zeros((2 * nc, BLK), f32)
    f_num[...] = jnp.zeros_like(f_num)
    m_num[...] = jnp.zeros_like(m_num)

    def visit(i, _):
        cell = todo[i]
        a, j = lax.div(cell, NZ), lax.rem(cell, NZ)
        key = f_tile(f_all, a, 0) * jnp.asarray(ROOT, bf16)
        valt = f_tile(f_all, a, 1)
        other, othert = m_key[j], m_valt[j]

        def side(scores, stat, row, count, num, at_block, h, weights):
            before = stat[pl.ds(row, 1), :]
            now = jnp.maximum(before, jnp.max(scores, axis=0, keepdims=True))
            fade = jnp.exp(before - now)
            part = jnp.exp(scores - now)
            stat[pl.ds(row, 1), :] = now
            sums = pl.ds(row + count, 1)
            stat[sums, :] = stat[sums, :] * fade + jnp.sum(part, axis=0, keepdims=True)
            rows = slice(h * DH, (h + 1) * DH)
            num[at_block, rows] = num[at_block, rows] * fade + nn(weights[rows], part.astype(bf16))

        for h in range(HEADS):
            own = of_head(key, h)
            side(nt(other, own), r_stat, h * NA + a, nr, f_num, a, h, othert)
            side(nt(own, other), c_stat, h * NZ + j, nc, m_num, j, h, valt)
        return 0

    lax.fori_loop(0, total, visit, 0)
    for a in range(NA):
        start = (2 * FB + a % FB) * BLK
        gradt = f_all[a // FB, start : start + BLK, :].astype(f32).T
        for h in range(HEADS):
            rows = slice(h * DH, (h + 1) * DH)
            row = 2 * nr + h * NA + a
            r_stat[row : row + 1] = jnp.sum(gradt[rows] * f_num[a, rows], axis=0, keepdims=True)
    for j in range(NZ):
        for h in range(HEADS):
            rows = slice(h * DH, (h + 1) * DH)
            row = 2 * nc + h * NZ + j
            c_stat[row : row + 1] = jnp.sum(m_gradt[j, rows] * m_num[j, rows], axis=0, keepdims=True)


def merge(parts, own, n):
    top = functools.reduce(jnp.maximum, [p[0:n] for p in parts])
    fades = [jnp.exp(p[0:n] - top) for p in parts]
    total = functools.reduce(jnp.add, [w * p[n : 2 * n] for w, p in zip(fades, parts)])
    delta = functools.reduce(jnp.add, [w * p[2 * n :] for w, p in zip(fades, parts)])
    safe = jnp.where(total > 0, total, 1.0)
    return top, safe, delta / safe, jnp.exp(own[0:n] - top) / safe


def backward_kernel(at, todo, f_all, r_own, r_all, c_own, f_num, m_num, *refs):
    m_in, c_in = refs[:NZ], refs[NZ : 2 * NZ - 1]
    f_out = refs[2 * NZ - 1]
    m_out = refs[2 * NZ : 3 * NZ]
    (m_key, m_keyt, m_val, m_grad, m_gradt, b_max, b_delta, r_max, r_inv, r_delta, d_rf, d_vf, d_rm, d_vm) = refs[3 * NZ :]
    z = at[0]
    nr, nc = HEADS * NA, HEADS * NZ
    top, total, delta, r_own_w = merge([r_all.at[p] for p in range(NG)], r_own, nr)
    r_max[...] = top
    r_inv[...] = 1.0 / total
    r_delta[...] = delta
    top, total, delta, c_own_w = merge([c_own, *c_in], c_own, nc)
    delta = delta / total
    pad = jnp.zeros((BLK - 3 * nc, BLK), f32)
    down = jnp.concatenate([top, total, delta, pad], axis=0).T
    b_total = []
    for j in range(NZ):
        for h in range(HEADS):
            k = h * NZ + j
            b_max[j, h] = jnp.broadcast_to(down[:, k : k + 1], (BLK, BLK))
            k += 2 * nc
            b_delta[j, h] = jnp.broadcast_to(down[:, k : k + 1], (BLK, BLK))
        k = nc + j
        b_total.append(
            jnp.where(
                head_mask(0),
                jnp.broadcast_to(down[:, k : k + 1], (BLK, BLK)),
                jnp.broadcast_to(down[:, k + NZ : k + NZ + 1], (BLK, BLK)),
            )
        )
    for s in range(NZ):
        j = lax.rem(z - s + NZ, NZ)
        m_key[j] = m_in[s][0:BLK]
        m_keyt[j] = (m_in[s][0:BLK].astype(f32) * ROOT).T.astype(bf16)
        m_val[j] = m_in[s][BLK : 2 * BLK]
        m_grad[j] = m_in[s][2 * BLK : 3 * BLK]
    for j in range(NZ):
        scaled = m_grad[j].astype(f32) / b_total[j]
        m_grad[j] = scaled.astype(bf16)
        m_gradt[j] = m_grad[j].astype(f32).T.astype(bf16)
    for ref in (d_rf, d_vf, d_rm, d_vm):
        ref[...] = jnp.zeros_like(ref)

    def visit(i, _):
        cell = todo[i]
        a, j = lax.div(cell, NZ), lax.rem(cell, NZ)
        key = f_tile(f_all, a, 0) * jnp.asarray(ROOT, bf16)
        valt = f_tile(f_all, a, 1)
        grad = f_tile(f_all, a, 2)
        other, other_val, scaled = m_key[j], m_val[j], m_grad[j]
        keys, grads, dscores, attns = [], [], [], []
        for h in range(HEADS):
            rows = slice(h * DH, (h + 1) * DH)
            row = pl.ds(h * NA + a, 1)
            own, own_grad = of_head(key, h), of_head(grad, h)
            scores = nt(other, own)
            attn = jnp.exp(scores - r_max[row, :]) * r_inv[row, :]
            col = jnp.exp(scores - b_max[j, h])
            dscore = attn * (nt(other_val, own_grad) - r_delta[row, :])
            dscore = dscore + col * (nn(of_head(scaled, h), valt) - b_delta[j, h])
            dscore = dscore.astype(bf16)
            d_rf[a, rows] += nn(m_keyt[j, rows], dscore)
            d_vf[a, rows] += nn(m_gradt[j, rows], col.astype(bf16))
            keys.append(own)
            grads.append(own_grad)
            dscores.append(dscore)
            attns.append(attn.astype(bf16))
        d_rm[j] += nn(jnp.concatenate(dscores, axis=1), jnp.concatenate(keys, axis=0))
        d_vm[j] += nn(jnp.concatenate(attns, axis=1), jnp.concatenate(grads, axis=0))
        return 0

    lax.fori_loop(0, todo[NA * NZ], visit, 0)
    for a in range(NA):
        base = (a % FB) * 3 * BLK
        for h in range(HEADS):
            rows = slice(h * DH, (h + 1) * DH)
            w = r_own_w[h * NA + a : h * NA + a + 1]
            f_out[a // FB, base + h * DH : base + (h + 1) * DH] = (f_num[a, rows] * w).astype(bf16)
        f_out[a // FB, base + BLK : base + 2 * BLK] = d_rf[a].astype(bf16)
        f_out[a // FB, base + 2 * BLK : base + 3 * BLK] = d_vf[a].astype(bf16)
    for j in range(NZ):
        for h in range(HEADS):
            rows = slice(h * DH, (h + 1) * DH)
            w = c_own_w[h * NZ + j : h * NZ + j + 1]
            m_num[j, rows] = m_num[j, rows] * w
    for s in range(NZ):
        j = lax.rem(z + s, NZ)
        m_out[s][0:BLK] = m_num[j].astype(bf16)
        m_out[s][BLK : 2 * BLK] = d_rm[j].astype(bf16)
        m_out[s][2 * BLK : 3 * BLK] = d_vm[j].astype(bf16)


def finish_kernel(f_parts, x, w_rf, w_vf, w_rm, w_vm, *refs):
    m_parts = refs[:NZ]
    fluid_out, metal_out, dx, wg = refs[NZ:]
    f_sum = functools.reduce(jnp.add, [f_parts[p].astype(f32) for p in range(NG)])
    m_sum = functools.reduce(jnp.add, [p[...].astype(f32) for p in m_parts])
    rf, vf = [], []
    for i in range(FB):
        base = i * 3 * BLK
        fluid_out[i * BLK : (i + 1) * BLK] = f_sum[base : base + BLK].T.astype(bf16)
        rf.append(f_sum[base + BLK : base + 2 * BLK].T.astype(bf16))
        vf.append(f_sum[base + 2 * BLK : base + 3 * BLK].T.astype(bf16))
    rf, vf = jnp.concatenate(rf, axis=0), jnp.concatenate(vf, axis=0)
    metal_out[...] = m_sum[0:BLK].T.astype(bf16)
    rm, vm = m_sum[BLK : 2 * BLK].astype(bf16), m_sum[2 * BLK :].astype(bf16)
    split = FB * BLK
    for i in range(NM):
        rows = slice(i * BLK, (i + 1) * BLK)
        dx[i, 0:split] = (nt(rf, w_rf[rows]) + nt(vf, w_vf[rows])).astype(dx.dtype)
        dx[i, split:] = (nt(rm, w_rm[rows]) + nt(vm, w_vm[rows])).astype(dx.dtype)
        fluid, metal = x[i, 0:split], x[i, split:]
        wg[0, rows] = tn(fluid, rf)
        wg[1, rows] = tn(fluid, vf)
        wg[2, rows] = tn(metal, rm)
        wg[3, rows] = tn(metal, vm)


def call(kernel, out, args, smem=0, scratch=(), smem_outs=(), aliases=None):
    out_specs = [SMEM if i in smem_outs else VMEM for i in range(len(out))]
    return pl.pallas_call(
        kernel,
        out_shape=[jax.ShapeDtypeStruct(*o) for o in out],
        in_specs=[SMEM] * smem + [VMEM] * (len(args) - smem),
        out_specs=out_specs,
        scratch_shapes=[pltpu.VMEM(*s) for s in scratch],
        input_output_aliases=aliases or {},
        compiler_params=PARAMS,
    )(*args)


def shift(value, axis, n, s):
    return lax.ppermute(value, axis, [(i, (i + s) % n) for i in range(n)])


def sum_over(a, axis, n):
    i = lax.axis_index(axis)
    parts = a.reshape((n, a.shape[0] // n) + a.shape[1:])
    total = lax.dynamic_index_in_dim(parts, i, 0, False)
    for s in range(1, n):
        total = total + shift(lax.dynamic_index_in_dim(parts, (i + s) % n, 0, False), axis, n, s)
    return total


def spread_over(a, axis, n):
    i = lax.axis_index(axis)
    out = jnp.zeros((n,) + a.shape, a.dtype)
    out = lax.dynamic_update_index_in_dim(out, a, i, 0)
    for s in range(1, n):
        out = lax.dynamic_update_index_in_dim(out, shift(a, axis, n, s), (i - s) % n, 0)
    return out.reshape((n * a.shape[0],) + a.shape[1:])


def body(fluid_x, metal_x, w_rf, w_vf, w_rm, w_vm, fluid_grad, metal_grad, pair_list, pair_count):
    weights = (w_rf, w_vf, w_rm, w_vm)
    z = lax.axis_index("z")
    at = z.reshape(1)
    tokens = jnp.concatenate([fluid_x, metal_x], axis=0)
    x = lax.all_gather(tokens, "m", axis=0)
    f_pay, m_pay = call(
        project_kernel,
        [((F_ROWS, BLK), bf16), ((M_ROWS, BLK), bf16)],
        [pair_count, x, *weights, fluid_grad, metal_grad, pair_list],
        smem=1,
    )
    f_all = lax.all_gather(f_pay, XC, axis=0)
    m_all = [m_pay] + [shift(m_pay, "z", NZ, s) for s in range(1, NZ)]
    table = f_all[:, 3 * FB * BLK, :].reshape(NA, NX, NZ, NC)
    table = lax.dynamic_index_in_dim(table, lax.axis_index("x"), 1, False)
    table = lax.dynamic_index_in_dim(table, lax.axis_index("c"), 2, False)
    live = (table.reshape(NA * NZ) > 0).astype(jnp.int32)
    block = (BLK, BLK)
    r_own, c_own, f_num, m_num, todo = call(
        forward_kernel,
        [
            ((3 * HEADS * NA, BLK), f32),
            ((3 * HEADS * NZ, BLK), f32),
            ((NA, *block), f32),
            ((NZ, *block), f32),
            ((NA * NZ + 8,), jnp.int32),
        ],
        [at, live, f_all, *m_all],
        smem=2,
        scratch=[((NZ, *block), bf16), ((NZ, *block), bf16), ((NZ, *block), f32)],
        smem_outs=(4,),
    )
    r_all = lax.all_gather(r_own, XC, axis=0)
    c_all = [shift(c_own, "z", NZ, s) for s in range(1, NZ)]
    tile_b, tile_f = ((NZ, *block), bf16), ((NZ, HEADS, *block), f32)
    f_part, *m_part = call(
        backward_kernel,
        [((NG, 3 * FB * BLK, BLK), bf16)] + [((M_ROWS, BLK), bf16)] * NZ,
        [at, todo, f_all, r_own, r_all, c_own, f_num, m_num, *m_all, *c_all],
        smem=2,
        scratch=[tile_b] * 5
        + [tile_f] * 2
        + [((HEADS * NA, BLK), f32)] * 3
        + [((NA, *block), f32)] * 2
        + [((NZ, *block), f32)] * 2,
    )
    f_part = lax.all_to_all(f_part, XC, 0, 0)
    m_part = [m_part[0]] + [shift(m_part[s], "z", NZ, s) for s in range(1, NZ)]
    fluid_out, metal_out, dx, wg = call(
        finish_kernel,
        [
            ((FB * BLK, BLK), bf16),
            ((BLK, BLK), bf16),
            ((NM, (FB + 1) * BLK, BLK), bf16),
            ((4, NM * BLK, BLK), f32),
        ],
        [f_part, x, *weights, *m_part],
    )
    dx = jnp.sum(lax.all_to_all(dx, "m", 0, 0).astype(f32), axis=0).astype(bf16)
    wg = wg.reshape(4 * NM * BLK, BLK)
    wg = sum_over(sum_over(sum_over(wg, "c", NC), "x", NX), "z", NZ)
    wg = spread_over(spread_over(spread_over(wg, "z", NZ), "x", NX), "c", NC)
    return fluid_out, metal_out, dx[: FB * BLK], dx[FB * BLK :], wg.reshape(4, NM * BLK, BLK)


def solution(mesh):
    grid = Mesh(mesh.devices.reshape(NX, NZ, NC, NM), ("x", "z", "c", "m"))
    tokens, weight = P(FLUID, "m"), P(None, "m")
    return jax.shard_map(
        body,
        mesh=grid,
        in_specs=(tokens, tokens, weight, weight, weight, weight, tokens, tokens, P(FLUID, None), P(FLUID)),
        out_specs=(tokens, tokens, tokens, tokens, P(None, None, "m")),
        check_vma=False,
    )
```

```python
import functools

import jax
import jax.numpy as jnp
from jax import lax
from jax.experimental import pallas as pl
from jax.experimental.pallas import tpu as pltpu
from jax.sharding import Mesh, PartitionSpec as P

BLK = 128
HEADS = 2
DH = 64
NX, NZ, NC, NM = 4, 8, 2, 4
NG = NX * NC
FB = 2
NA = NG * FB
LOWEST = -1e30
ROOT = 0.125
XC = ("x", "c")
FLUID = ("x", "z", "c")
F_ROWS = 3 * FB * BLK + 16
M_ROWS = 3 * BLK
f32, bf16 = jnp.float32, jnp.bfloat16
PARAMS = pltpu.CompilerParams(vmem_limit_bytes=24 * 2**20)
VMEM = pl.BlockSpec(memory_space=pltpu.VMEM)
SMEM = pl.BlockSpec(memory_space=pltpu.SMEM)
AT_ONCE = 4
CELL = 16


def nn(a, b):
    return lax.dot_general(a, b, (((1,), (0,)), ((), ())), preferred_element_type=f32)


def nt(a, b):
    return lax.dot_general(a, b, (((1,), (1,)), ((), ())), preferred_element_type=f32)


def tn(a, b):
    return lax.dot_general(a, b, (((0,), (0,)), ((), ())), preferred_element_type=f32)


def head_mask(h):
    lane = lax.broadcasted_iota(jnp.int32, (BLK, BLK), 1)
    return lane < DH if h == 0 else lane >= DH


def of_head(tile, h):
    return jnp.where(head_mask(h), tile, jnp.zeros_like(tile))


def project_kernel(at, count, *refs):
    x, w, refs = refs[:NM], refs[NM : NM + 4], refs[NM + 4 :]
    f_grad, m_grad, pairs, f_pay, m_pay = refs
    f_pay[2 * FB * BLK : 3 * FB * BLK] = f_grad[...]
    m_pay[2 * BLK :] = m_grad[...]
    m = at[3]
    slots = pairs.shape[0]
    code = pairs[:, 0:1] * (NX * NZ * NC) + pairs[:, 1:2]
    lane = lax.broadcasted_iota(jnp.int32, (slots, BLK), 1)
    slot = lax.broadcasted_iota(jnp.int32, (slots, BLK), 0)
    hit = jnp.where((code == lane) & (slot < count[0]), 1.0, 0.0)
    table = jnp.max(hit, axis=0, keepdims=True)
    f_pay[3 * FB * BLK :] = jnp.broadcast_to(table, (16, BLK)).astype(bf16)

    def project(rows, k):
        total = None
        for s in range(NM):
            start = pl.multiple_of(lax.rem(m - s + NM, NM) * BLK, BLK)
            part = nn(x[s][rows], w[k][pl.ds(start, BLK), :])
            total = part if total is None else total + part
        return total

    fluid, metal = slice(0, FB * BLK), slice(FB * BLK, FB * BLK + BLK)
    f_pay[0 : FB * BLK] = project(fluid, 0).astype(bf16)
    values = project(fluid, 1).astype(bf16)
    for i in range(FB):
        start = (FB + i) * BLK
        f_pay[start : start + BLK] = values[i * BLK : (i + 1) * BLK].T
    m_pay[0:BLK] = project(metal, 2).astype(bf16)
    m_pay[BLK : 2 * BLK] = project(metal, 3).astype(bf16)


def bring(at, m_in, m_all):
    for s in range(NZ):
        m_all[lax.rem(at[1] - s + NZ, NZ)] = m_in[s][...]


def f_tile(f_all, a, part):
    start = pl.multiple_of(part * FB * BLK + lax.rem(a, FB) * BLK, BLK)
    return f_all[jnp.minimum(lax.div(a, FB), NG - 1), pl.ds(start, BLK), :]


def spread(tile, k):
    return jnp.broadcast_to(tile[:, k : k + 1], (BLK, BLK))


def pair_at(todo, i):
    cell = todo[i]
    return lax.div(cell, CELL), lax.rem(cell, CELL)


def forward_kernel(at, live, f_all, *refs):
    m_in, refs = refs[:NZ], refs[NZ:]
    r_stat, c_stat, f_num, m_num, todo = refs[:5]
    m_all, m_valt, f_acc, m_acc, r_max, r_sum, c_top, c_sum = refs[5:]
    bring(at, m_in, m_all)

    def list_step(a, n):
        for j in range(NZ):
            todo[n] = a * CELL + j
            n = n + live[a * NZ + j]
        return n

    total = lax.fori_loop(0, NA, list_step, 0)
    for k in range(AT_ONCE):
        todo[total + k] = NA * CELL + NZ
    turns = lax.div(total + AT_ONCE - 1, AT_ONCE)
    todo[NA * NZ + 8] = turns
    for ref in (r_max, c_top):
        ref[...] = jnp.full(ref.shape, LOWEST, f32)
    for ref in (r_sum, c_sum, f_acc, m_acc):
        ref[...] = jnp.zeros_like(ref)

    def scores_of(a, j):
        key = f_tile(f_all, a, 0) * jnp.asarray(ROOT, bf16)
        return [nt(m_all[j, 0:BLK], of_head(key, h)) for h in range(HEADS)]

    def max_step(i, _):
        tops = []
        for k in range(AT_ONCE):
            a, j = pair_at(todo, i * AT_ONCE + k)
            for h, scores in enumerate(scores_of(a, j)):
                tops.append((h, a, j, scores, jnp.max(scores, axis=0, keepdims=True)))
        for h, a, j, scores, top in tops:
            r_max[h, pl.ds(a, 1), :] = jnp.maximum(r_max[h, pl.ds(a, 1), :], top)
            c_top[j, h] = jnp.maximum(c_top[j, h], scores)
        return 0

    lax.fori_loop(0, turns, max_step, 0)
    lane = lax.broadcasted_iota(jnp.int32, (BLK, BLK), 1)
    down = jnp.zeros((BLK, BLK), f32)
    for j in range(NZ):
        m_valt[j] = m_all[j, BLK : 2 * BLK].T
        for h in range(HEADS):
            top = jnp.broadcast_to(jnp.max(c_top[j, h], axis=1, keepdims=True), (BLK, BLK))
            c_top[j, h] = top
            down = jnp.where(lane == h * NZ + j, top, down)

    def sum_step(i, _):
        f_adds, m_adds = [], []
        for k in range(AT_ONCE):
            a, j = pair_at(todo, i * AT_ONCE + k)
            valt, othert = f_tile(f_all, a, 1), m_valt[j]
            parts = []
            for h, scores in enumerate(scores_of(a, j)):
                rows = slice(h * DH, (h + 1) * DH)
                part = jnp.exp(scores - r_max[h, pl.ds(a, 1), :])
                f_adds.append((h, a, jnp.sum(part, axis=0, keepdims=True), nn(othert[rows], part.astype(bf16))))
                parts.append(jnp.exp(scores - c_top[j, h]))
            left = jnp.concatenate([p.astype(bf16) for p in parts], axis=1)
            zero = jnp.zeros((DH, BLK), bf16)
            right = jnp.concatenate(
                [jnp.concatenate([valt[:DH], zero], axis=0), jnp.concatenate([zero, valt[DH:]], axis=0)], axis=1
            )
            m_adds.append((j, parts, nt(left, right)))
        for h, a, total, num in f_adds:
            r_sum[h, pl.ds(a, 1), :] += total
            f_acc[a, h * DH : (h + 1) * DH] += num
        for j, parts, num in m_adds:
            for h in range(HEADS):
                c_sum[j, h] += parts[h]
            m_acc[j] += num
        return 0

    lax.fori_loop(0, turns, sum_step, 0)
    for h in range(HEADS):
        for k, ref in enumerate((r_max, r_sum)):
            r_stat[(k * HEADS + h) * NA : (k * HEADS + h + 1) * NA] = ref[h, 0:NA]
    f_num[...] = f_acc[0:NA]
    m_num[...] = m_acc[0:NZ]
    for a in range(NA):
        start = (2 * FB + a % FB) * BLK
        gradt = f_all[a // FB, start : start + BLK, :].T
        for h in range(HEADS):
            rows = slice(h * DH, (h + 1) * DH)
            row = (2 * HEADS + h) * NA + a
            r_stat[row : row + 1] = jnp.sum(gradt[rows].astype(f32) * f_acc[a, rows], axis=0, keepdims=True)
    nc = HEADS * NZ
    for j in range(NZ):
        product = m_all[j, 2 * BLK : 3 * BLK].astype(f32) * m_acc[j]
        for h in range(HEADS):
            k = h * NZ + j
            down = jnp.where(lane == nc + k, jnp.sum(c_sum[j, h], axis=1, keepdims=True), down)
            down = jnp.where(lane == 2 * nc + k, jnp.sum(of_head(product, h), axis=1, keepdims=True), down)
    across = down.T[0 : 3 * nc]
    c_stat[...] = across


def merge(parts, own, n):
    top = functools.reduce(jnp.maximum, [p[0:n] for p in parts])
    fades = [jnp.exp(p[0:n] - top) for p in parts]
    total = functools.reduce(jnp.add, [w * p[n : 2 * n] for w, p in zip(fades, parts)])
    delta = functools.reduce(jnp.add, [w * p[2 * n : 3 * n] for w, p in zip(fades, parts)])
    safe = jnp.where(total > 0, total, 1.0)
    return top, safe, delta / safe, jnp.exp(own[0:n] - top) / safe


def backward_kernel(at, todo, f_all, *refs):
    m_in, refs = refs[:NZ], refs[NZ:]
    r_in, c_in, f_num, m_num, refs = refs[:NG], refs[NG], refs[NG + 1], refs[NG + 2], refs[NG + 3 :]
    f_out, m_out, refs = refs[:NG], refs[NG : NG + NZ], refs[NG + NZ :]
    m_all, m_keyt, m_grad, m_gradt, b_max, b_delta, r_max, r_inv, r_delta, d_rf, d_vf, d_rm, d_vm, out_num = refs
    bring(at, m_in, m_all)
    nr, nc = HEADS * NA, HEADS * NZ
    for ref in (d_rf, d_vf, d_rm, d_vm):
        ref[...] = jnp.zeros_like(ref)
    top, total, delta, r_own = merge(r_in, r_in[0], nr)
    inv = 1.0 / total
    for h in range(HEADS):
        rows = slice(h * NA, (h + 1) * NA)
        r_max[h, 0:NA] = top[rows]
        r_inv[h, 0:NA] = inv[rows]
        r_delta[h, 0:NA] = delta[rows]
    top, total, delta, c_fade = merge([c_in.at[p] for p in range(NZ)], c_in.at[0], nc)
    delta = delta / total
    pad = jnp.zeros((BLK - 4 * nc, BLK), f32)
    down = jnp.concatenate([top, total, delta, c_fade, pad], axis=0).T

    def both_heads(k):
        return jnp.where(head_mask(0), spread(down, k), spread(down, k + NZ))

    for j in range(NZ):
        for h in range(HEADS):
            b_max[j, h] = spread(down, h * NZ + j)
            b_delta[j, h] = spread(down, 2 * nc + h * NZ + j)
        m_keyt[j] = (m_all[j, 0:BLK] * jnp.asarray(ROOT, bf16)).T
        scaled = (m_all[j, 2 * BLK : 3 * BLK].astype(f32) / both_heads(nc + j)).astype(bf16)
        m_grad[j] = scaled
        m_gradt[j] = scaled.T

    def visit(i, _):
        f_adds, m_adds = [], []
        for n in range(AT_ONCE):
            a, j = pair_at(todo, i * AT_ONCE + n)
            row = pl.ds(a, 1)
            key = f_tile(f_all, a, 0) * jnp.asarray(ROOT, bf16)
            valt = f_tile(f_all, a, 1)
            grad = f_tile(f_all, a, 2)
            other, other_val, scaled = m_all[j, 0:BLK], m_all[j, BLK : 2 * BLK], m_grad[j]
            keys, grads, dscores, attns = [], [], [], []
            for h in range(HEADS):
                rows = slice(h * DH, (h + 1) * DH)
                own, own_grad = of_head(key, h), of_head(grad, h)
                scores = nt(other, own)
                attn = jnp.exp(scores - r_max[h, row, :]) * r_inv[h, row, :]
                col = jnp.exp(scores - b_max[j, h])
                dscore = attn * (nt(other_val, own_grad) - r_delta[h, row, :])
                dscore = dscore + col * (nn(of_head(scaled, h), valt) - b_delta[j, h])
                dscore = dscore.astype(bf16)
                f_adds.append((a, rows, nn(m_keyt[j, rows], dscore), nn(m_gradt[j, rows], col.astype(bf16))))
                keys.append(own)
                grads.append(own_grad)
                dscores.append(dscore)
                attns.append(attn.astype(bf16))
            rm = nn(jnp.concatenate(dscores, axis=1), jnp.concatenate(keys, axis=0))
            vm = nn(jnp.concatenate(attns, axis=1), jnp.concatenate(grads, axis=0))
            m_adds.append((j, rm, vm))
        for a, rows, rf, vf in f_adds:
            d_rf[a, rows] += rf
            d_vf[a, rows] += vf
        for j, rm, vm in m_adds:
            d_rm[j] += rm
            d_vm[j] += vm
        return 0

    lax.fori_loop(0, todo[NA * NZ + 8], visit, 0)
    for a in range(NA):
        for h in range(HEADS):
            rows = slice(h * DH, (h + 1) * DH)
            out_num[a, rows] = f_num[a, rows] * r_own[h * NA + a : h * NA + a + 1]
    for i in range(NG):
        s, k = i % NX, i // NX
        f = lax.rem(at[0] + s, NX) * NC + lax.rem(at[2] + k, NC)
        for b in range(FB):
            base = b * 3 * BLK
            f_out[i][base : base + BLK] = out_num[f * FB + b].astype(bf16)
            f_out[i][base + BLK : base + 2 * BLK] = d_rf[f * FB + b].astype(bf16)
            f_out[i][base + 2 * BLK : base + 3 * BLK] = d_vf[f * FB + b].astype(bf16)
    for j in range(NZ):
        b_max[j, 0] = m_num[j] * both_heads(3 * nc + j)
    for s in range(NZ):
        j = lax.rem(at[1] + s, NZ)
        m_out[s][0:BLK] = b_max[j, 0].astype(bf16)
        m_out[s][BLK : 2 * BLK] = d_rm[j].astype(bf16)
        m_out[s][2 * BLK : 3 * BLK] = d_vm[j].astype(bf16)


def finish_kernel(at, *refs):
    x, weights, refs = refs[:NM], refs[NM : NM + 4], refs[NM + 4 :]
    f_parts, m_parts, refs = refs[: NX + 1], refs[NX + 1 : NX + 1 + NZ], refs[NX + 1 + NZ :]
    fluid_out, metal_out, wg, dx = refs[0], refs[1], refs[2], refs[3:]
    w_rf, w_vf, w_rm, w_vm = weights
    f_sum = functools.reduce(jnp.add, [p[...].astype(f32) for p in f_parts])
    m_sum = functools.reduce(jnp.add, [p[...].astype(f32) for p in m_parts])
    rf, vf = [], []
    for i in range(FB):
        base = i * 3 * BLK
        fluid_out[i * BLK : (i + 1) * BLK] = f_sum[base : base + BLK].T.astype(bf16)
        rf.append(f_sum[base + BLK : base + 2 * BLK].T.astype(bf16))
        vf.append(f_sum[base + 2 * BLK : base + 3 * BLK].T.astype(bf16))
    rf, vf = jnp.concatenate(rf, axis=0), jnp.concatenate(vf, axis=0)
    metal_out[...] = m_sum[0:BLK].astype(bf16)
    rm, vm = m_sum[BLK : 2 * BLK].astype(bf16), m_sum[2 * BLK :].astype(bf16)
    split = FB * BLK
    for i in range(NM):
        rows = pl.ds(pl.multiple_of(lax.rem(at[3] + i, NM) * BLK, BLK), BLK)
        dx[i][0:split] = (nt(rf, w_rf[rows, :]) + nt(vf, w_vf[rows, :])).astype(bf16)
        dx[i][split:] = (nt(rm, w_rm[rows, :]) + nt(vm, w_vm[rows, :])).astype(bf16)
        fluid, metal = x[i][0:split], x[i][split:]
        start = lax.rem(at[3] - i + NM, NM) * BLK
        for k, (left, right) in enumerate(((fluid, rf), (fluid, vf), (metal, rm), (metal, vm))):
            wg[pl.ds(pl.multiple_of(k * NM * BLK + start, BLK), BLK), :] = tn(left, right)


def total_kernel(at, *refs):
    parts, out, place = refs[:NZ], refs[NZ], refs[NZ + 1]
    for s in range(NZ):
        place[lax.rem(at[1] - s + NZ, NZ)] = parts[s][...]
    out[...] = functools.reduce(jnp.add, [place[s].astype(f32) for s in range(NZ)])


def add_kernel(*refs):
    parts, fluid, metal = refs[:NM], refs[NM], refs[NM + 1]
    total = functools.reduce(jnp.add, [p[...].astype(f32) for p in parts]).astype(bf16)
    fluid[...] = total[: FB * BLK]
    metal[...] = total[FB * BLK :]


def pack_kernel(fluid, metal, out):
    out[0 : FB * BLK] = fluid[...]
    out[FB * BLK :] = metal[...]


def call(kernel, out, args, scalars, scratch=(), smem_outs=()):
    return pl.pallas_call(
        kernel,
        out_shape=[jax.ShapeDtypeStruct(*o) for o in out],
        in_specs=[SMEM] * scalars + [VMEM] * (len(args) - scalars),
        out_specs=[SMEM if i in smem_outs else VMEM for i in range(len(out))],
        scratch_shapes=scratch,
        compiler_params=PARAMS,
    )(*args)


def shift(value, axis, n, s):
    return lax.ppermute(value, axis, [(i, (i + s) % n) for i in range(n)])


def pieces(value, axis, n):
    return [value] + [shift(value, axis, n, s) for s in range(1, n)]


def group_pieces(value):
    near = pieces(value, "x", NX)
    return near + [shift(p, "c", NC, 1) for p in near]


def doubled(value, axis, n):
    value, step = value[None], 1
    while step < n:
        other = lax.ppermute(value, axis, [(i, i ^ step) for i in range(n)])
        value, step = jnp.concatenate([value, other], axis=0), 2 * step
    return value


def sum_over(a, axis, n, dtype):
    i = lax.axis_index(axis)
    parts = a.reshape((n, a.shape[0] // n) + a.shape[1:])
    total = lax.dynamic_index_in_dim(parts, i, 0, False)
    for s in range(1, n):
        part = lax.dynamic_index_in_dim(parts, (i + s) % n, 0, False)
        total = total + shift(part.astype(dtype), axis, n, s).astype(f32)
    return total


def spread_over(a, axis, n):
    i = lax.axis_index(axis)
    out = jnp.zeros((n,) + a.shape, a.dtype)
    for s, piece in enumerate(pieces(a, axis, n)):
        out = lax.dynamic_update_index_in_dim(out, piece, (i - s) % n, 0)
    return out.reshape((n * a.shape[0],) + a.shape[1:])


def body(fluid_x, metal_x, w_rf, w_vf, w_rm, w_vm, fluid_grad, metal_grad, pair_list, pair_count):
    weights = [w_rf, w_vf, w_rm, w_vm]
    at = jnp.stack([lax.axis_index(k) for k in ("x", "z", "c", "m")]).astype(jnp.int32)
    (x,) = call(pack_kernel, [(((FB + 1) * BLK, BLK), bf16)], [fluid_x, metal_x], 0)
    x = pieces(x, "m", NM)
    f_pay, m_pay = call(
        project_kernel,
        [((F_ROWS, BLK), bf16), ((M_ROWS, BLK), bf16)],
        [at, pair_count, *x, *weights, fluid_grad, metal_grad, pair_list],
        2,
    )
    f_in = lax.all_gather(f_pay, XC, axis=0)
    m_in = pieces(m_pay, "z", NZ)
    table = f_in[:, 3 * FB * BLK].reshape(NA, NX, NZ, NC)
    table = lax.dynamic_index_in_dim(table, at[0], 1, False)
    table = lax.dynamic_index_in_dim(table, at[2], 2, False)
    live = (table.reshape(NA * NZ) > 0).astype(jnp.int32)
    block = (BLK, BLK)
    moved = pltpu.VMEM((NZ + 1, M_ROWS, BLK), bf16)
    f_acc, m_acc = pltpu.VMEM((NA + 1, *block), f32), pltpu.VMEM((NZ + 1, *block), f32)
    m_tiles = pltpu.VMEM((NZ + 1, *block), bf16)
    r_rows = pltpu.VMEM((HEADS, NA + 8, BLK), f32)
    tiles = pltpu.VMEM((NZ + 1, HEADS, *block), f32)
    r_own, c_own, f_num, m_num, todo = call(
        forward_kernel,
        [
            ((3 * HEADS * NA, BLK), f32),
            ((3 * HEADS * NZ, BLK), f32),
            ((NA, *block), f32),
            ((NZ, *block), f32),
            ((NA * NZ + 16,), jnp.int32),
        ],
        [at, live, f_in, *m_in],
        2,
        [moved, m_tiles, f_acc, m_acc, r_rows, r_rows, tiles, tiles],
        smem_outs=(4,),
    )
    c_in = doubled(c_own, "z", NZ)
    r_in = group_pieces(r_own)
    out = call(
        backward_kernel,
        [((3 * FB * BLK, BLK), bf16)] * NG + [((M_ROWS, BLK), bf16)] * NZ,
        [at, todo, f_in, *m_in, *r_in, c_in, f_num, m_num],
        2,
        [moved, m_tiles, m_tiles, m_tiles, tiles, tiles, r_rows, r_rows, r_rows, f_acc, f_acc, m_acc, m_acc, f_acc],
    )
    f_out, m_out = out[:NG], out[NG:]
    came = [shift(p, "c", NC, 1) for p in f_out[NX:]]
    f_part = [f_out[0], came[0]]
    for s in range(1, NX):
        both = (f_out[s].astype(f32) + came[s].astype(f32)).astype(bf16)
        f_part.append(shift(both, "x", NX, s))
    m_part = [m_out[0]] + [shift(m_out[s], "z", NZ, s) for s in range(1, NZ)]
    fluid_out, metal_out, wg, *dx = call(
        finish_kernel,
        [
            ((FB * BLK, BLK), bf16),
            ((BLK, BLK), bf16),
            ((4 * NM * BLK, BLK), f32),
        ]
        + [(((FB + 1) * BLK, BLK), bf16)] * NM,
        [at, *x, *weights, *f_part, *m_part],
        1,
    )
    dx = [dx[0]] + [shift(dx[s], "m", NM, s) for s in range(1, NM)]
    wg = sum_over(sum_over(wg, "c", NC, f32), "x", NX, bf16)
    wg, dx = lax.optimization_barrier((wg, dx))
    (wg,) = call(
        total_kernel,
        [(wg.shape, f32)],
        [at, *pieces(wg.astype(bf16), "z", NZ)],
        1,
        [pltpu.VMEM((NZ, *wg.shape), bf16)],
    )
    wg = spread_over(spread_over(wg, "x", NX), "c", NC)
    fluid_dx, metal_dx = call(
        add_kernel, [((FB * BLK, BLK), bf16), ((BLK, BLK), bf16)], list(dx), 0
    )
    return fluid_out, metal_out, fluid_dx, metal_dx, wg.reshape(4, NM * BLK, BLK)


def solution(mesh):
    grid = Mesh(mesh.devices.reshape(NX, NZ, NC, NM), ("x", "z", "c", "m"))
    tokens, weight = P(FLUID, "m"), P(None, "m")
    return jax.shard_map(
        body,
        mesh=grid,
        in_specs=(tokens, tokens, weight, weight, weight, weight, tokens, tokens, P(FLUID, None), P(FLUID)),
        out_specs=(tokens, tokens, tokens, tokens, P(None, None, "m")),
        check_vma=False,
    )
```

```python
import functools

import jax
import jax.numpy as jnp
from jax import lax
from jax.experimental import pallas as pl
from jax.experimental.pallas import tpu as pltpu
from jax.sharding import Mesh, PartitionSpec as P

BLK = 128
HEADS = 2
DH = 64
NX, NZ, NC, NM = 4, 8, 2, 4
NG = NX * NC
FB = 2
NP = NZ // 2
WROWS = 4 * NM * BLK // NG
NA = NG * FB
LOWEST = -1e30
ROOT = 0.125
XC = ("x", "c")
FLUID = ("x", "z", "c")
F_ROWS = 3 * FB * BLK + 16
M_ROWS = 3 * BLK
f32, bf16 = jnp.float32, jnp.bfloat16
PARAMS = pltpu.CompilerParams(vmem_limit_bytes=24 * 2**20)
VMEM = pl.BlockSpec(memory_space=pltpu.VMEM)
SMEM = pl.BlockSpec(memory_space=pltpu.SMEM)
AT_ONCE = 4
CELL = 16


def nn(a, b):
    return lax.dot_general(a, b, (((1,), (0,)), ((), ())), preferred_element_type=f32)


def nt(a, b):
    return lax.dot_general(a, b, (((1,), (1,)), ((), ())), preferred_element_type=f32)


def tn(a, b):
    return lax.dot_general(a, b, (((0,), (0,)), ((), ())), preferred_element_type=f32)


def head_mask(h):
    lane = lax.broadcasted_iota(jnp.int32, (BLK, BLK), 1)
    return lane < DH if h == 0 else lane >= DH


def of_head(tile, h):
    return jnp.where(head_mask(h), tile, jnp.zeros_like(tile))


def project_kernel(at, count, *refs):
    x, w, refs = refs[:NM], refs[NM : NM + 4], refs[NM + 4 :]
    f_grad, m_grad, pairs, f_pay, m_pay = refs
    f_pay[2 * FB * BLK : 3 * FB * BLK] = f_grad[...]
    m_pay[2 * BLK :] = m_grad[...]
    m = at[3]
    slots = pairs.shape[0]
    code = pairs[:, 0:1] * (NX * NZ * NC) + pairs[:, 1:2]
    lane = lax.broadcasted_iota(jnp.int32, (slots, BLK), 1)
    slot = lax.broadcasted_iota(jnp.int32, (slots, BLK), 0)
    hit = jnp.where((code == lane) & (slot < count[0]), 1.0, 0.0)
    table = jnp.max(hit, axis=0, keepdims=True)
    f_pay[3 * FB * BLK :] = jnp.broadcast_to(table, (16, BLK)).astype(bf16)

    def project(rows, k):
        total = None
        for s in range(NM):
            start = pl.multiple_of(lax.rem(m - s + NM, NM) * BLK, BLK)
            part = nn(x[s][rows], w[k][pl.ds(start, BLK), :])
            total = part if total is None else total + part
        return total

    fluid, metal = slice(0, FB * BLK), slice(FB * BLK, FB * BLK + BLK)
    f_pay[0 : FB * BLK] = project(fluid, 0).astype(bf16)
    values = project(fluid, 1).astype(bf16)
    for i in range(FB):
        start = (FB + i) * BLK
        f_pay[start : start + BLK] = values[i * BLK : (i + 1) * BLK].T
    m_pay[0:BLK] = project(metal, 2).astype(bf16)
    m_pay[BLK : 2 * BLK] = project(metal, 3).astype(bf16)


def bring(at, m_in, m_all):
    for s in range(NZ):
        m_all[lax.rem(at[1] - s + NZ, NZ)] = m_in[s][...]


def f_tile(f_all, a, part):
    start = pl.multiple_of(part * FB * BLK + lax.rem(a, FB) * BLK, BLK)
    return f_all[jnp.minimum(lax.div(a, FB), NG - 1), pl.ds(start, BLK), :]


def spread(tile, k):
    return jnp.broadcast_to(tile[:, k : k + 1], (BLK, BLK))


def pair_at(todo, i):
    cell = todo[i]
    return lax.div(cell, CELL), lax.rem(cell, CELL)


def forward_kernel(at, live, f_all, *refs):
    m_in, refs = refs[:NZ], refs[NZ:]
    r_stat, c_stat, f_num, m_num, todo = refs[:5]
    m_all, m_valt, f_acc, m_acc, r_max, r_sum, c_top, c_sum = refs[5:]
    bring(at, m_in, m_all)

    def list_step(a, n):
        for j in range(NZ):
            todo[n] = a * CELL + j
            n = n + live[a * NZ + j]
        return n

    total = lax.fori_loop(0, NA, list_step, 0)
    for k in range(AT_ONCE):
        todo[total + k] = NA * CELL + NZ
    turns = lax.div(total + AT_ONCE - 1, AT_ONCE)
    todo[NA * NZ + 8] = turns
    for ref in (r_max, c_top):
        ref[...] = jnp.full(ref.shape, LOWEST, f32)
    for ref in (r_sum, c_sum, f_acc, m_acc):
        ref[...] = jnp.zeros_like(ref)

    def scores_of(a, j):
        key = f_tile(f_all, a, 0) * jnp.asarray(ROOT, bf16)
        return [nt(m_all[j, 0:BLK], of_head(key, h)) for h in range(HEADS)]

    def max_step(i, _):
        tops = []
        for k in range(AT_ONCE):
            a, j = pair_at(todo, i * AT_ONCE + k)
            for h, scores in enumerate(scores_of(a, j)):
                tops.append((h, a, j, scores, jnp.max(scores, axis=0, keepdims=True)))
        for h, a, j, scores, top in tops:
            r_max[h, pl.ds(a, 1), :] = jnp.maximum(r_max[h, pl.ds(a, 1), :], top)
            c_top[j, h] = jnp.maximum(c_top[j, h], scores)
        return 0

    lax.fori_loop(0, turns, max_step, 0)
    lane = lax.broadcasted_iota(jnp.int32, (BLK, BLK), 1)
    down = jnp.zeros((BLK, BLK), f32)
    for j in range(NZ):
        m_valt[j] = m_all[j, BLK : 2 * BLK].T
        for h in range(HEADS):
            top = jnp.broadcast_to(jnp.max(c_top[j, h], axis=1, keepdims=True), (BLK, BLK))
            c_top[j, h] = top
            down = jnp.where(lane == h * NZ + j, top, down)

    def sum_step(i, _):
        f_adds, m_adds = [], []
        for k in range(AT_ONCE):
            a, j = pair_at(todo, i * AT_ONCE + k)
            valt, othert = f_tile(f_all, a, 1), m_valt[j]
            parts = []
            for h, scores in enumerate(scores_of(a, j)):
                rows = slice(h * DH, (h + 1) * DH)
                part = jnp.exp(scores - r_max[h, pl.ds(a, 1), :])
                f_adds.append((h, a, jnp.sum(part, axis=0, keepdims=True), nn(othert[rows], part.astype(bf16))))
                parts.append(jnp.exp(scores - c_top[j, h]))
            left = jnp.concatenate([p.astype(bf16) for p in parts], axis=1)
            zero = jnp.zeros((DH, BLK), bf16)
            right = jnp.concatenate(
                [jnp.concatenate([valt[:DH], zero], axis=0), jnp.concatenate([zero, valt[DH:]], axis=0)], axis=1
            )
            m_adds.append((j, parts, nt(left, right)))
        for h, a, total, num in f_adds:
            r_sum[h, pl.ds(a, 1), :] += total
            f_acc[a, h * DH : (h + 1) * DH] += num
        for j, parts, num in m_adds:
            for h in range(HEADS):
                c_sum[j, h] += parts[h]
            m_acc[j] += num
        return 0

    lax.fori_loop(0, turns, sum_step, 0)
    for h in range(HEADS):
        for k, ref in enumerate((r_max, r_sum)):
            r_stat[(k * HEADS + h) * NA : (k * HEADS + h + 1) * NA] = ref[h, 0:NA]
    f_num[...] = f_acc[0:NA]
    m_num[...] = m_acc[0:NZ]
    for a in range(NA):
        start = (2 * FB + a % FB) * BLK
        gradt = f_all[a // FB, start : start + BLK, :].T
        for h in range(HEADS):
            rows = slice(h * DH, (h + 1) * DH)
            row = (2 * HEADS + h) * NA + a
            r_stat[row : row + 1] = jnp.sum(gradt[rows].astype(f32) * f_acc[a, rows], axis=0, keepdims=True)
    nc = HEADS * NZ
    for j in range(NZ):
        product = m_all[j, 2 * BLK : 3 * BLK].astype(f32) * m_acc[j]
        for h in range(HEADS):
            k = h * NZ + j
            down = jnp.where(lane == nc + k, jnp.sum(c_sum[j, h], axis=1, keepdims=True), down)
            down = jnp.where(lane == 2 * nc + k, jnp.sum(of_head(product, h), axis=1, keepdims=True), down)
    across = down.T[0 : 3 * nc]
    c_stat[...] = across


def merge(parts, own, n):
    top = functools.reduce(jnp.maximum, [p[0:n] for p in parts])
    fades = [jnp.exp(p[0:n] - top) for p in parts]
    total = functools.reduce(jnp.add, [w * p[n : 2 * n] for w, p in zip(fades, parts)])
    delta = functools.reduce(jnp.add, [w * p[2 * n : 3 * n] for w, p in zip(fades, parts)])
    safe = jnp.where(total > 0, total, 1.0)
    return top, safe, delta / safe, jnp.exp(own[0:n] - top) / safe


def backward_kernel(at, todo, f_all, *refs):
    m_in, refs = refs[:NZ], refs[NZ:]
    r_in, c_in, f_num, m_num, refs = refs[:NG], refs[NG], refs[NG + 1], refs[NG + 2], refs[NG + 3 :]
    f_keep, f_send, refs = refs[:NX], refs[NX], refs[NX + 1 :]
    m_keep, m_send, refs = refs[:NP], refs[NP], refs[NP + 1 :]
    m_all, m_keyt, m_grad, m_gradt, b_max, b_delta, r_max, r_inv, r_delta, d_rf, d_vf, d_rm, d_vm, out_num = refs
    bring(at, m_in, m_all)
    nr, nc = HEADS * NA, HEADS * NZ
    for ref in (d_rf, d_vf, d_rm, d_vm):
        ref[...] = jnp.zeros_like(ref)
    top, total, delta, r_own = merge(r_in, r_in[0], nr)
    inv = 1.0 / total
    for h in range(HEADS):
        rows = slice(h * NA, (h + 1) * NA)
        r_max[h, 0:NA] = top[rows]
        r_inv[h, 0:NA] = inv[rows]
        r_delta[h, 0:NA] = delta[rows]
    top, total, delta, c_fade = merge([c_in.at[p] for p in range(NZ)], c_in.at[0], nc)
    delta = delta / total
    pad = jnp.zeros((BLK - 4 * nc, BLK), f32)
    down = jnp.concatenate([top, total, delta, c_fade, pad], axis=0).T

    def both_heads(k):
        return jnp.where(head_mask(0), spread(down, k), spread(down, k + NZ))

    for j in range(NZ):
        for h in range(HEADS):
            b_max[j, h] = spread(down, h * NZ + j)
            b_delta[j, h] = spread(down, 2 * nc + h * NZ + j)
        m_keyt[j] = (m_all[j, 0:BLK] * jnp.asarray(ROOT, bf16)).T
        scaled = (m_all[j, 2 * BLK : 3 * BLK].astype(f32) / both_heads(nc + j)).astype(bf16)
        m_grad[j] = scaled
        m_gradt[j] = scaled.T

    def visit(i, _):
        f_adds, m_adds = [], []
        for n in range(AT_ONCE):
            a, j = pair_at(todo, i * AT_ONCE + n)
            row = pl.ds(a, 1)
            key = f_tile(f_all, a, 0) * jnp.asarray(ROOT, bf16)
            valt = f_tile(f_all, a, 1)
            grad = f_tile(f_all, a, 2)
            other, other_val, scaled = m_all[j, 0:BLK], m_all[j, BLK : 2 * BLK], m_grad[j]
            keys, grads, dscores, attns = [], [], [], []
            for h in range(HEADS):
                rows = slice(h * DH, (h + 1) * DH)
                own, own_grad = of_head(key, h), of_head(grad, h)
                scores = nt(other, own)
                attn = jnp.exp(scores - r_max[h, row, :]) * r_inv[h, row, :]
                col = jnp.exp(scores - b_max[j, h])
                dscore = attn * (nt(other_val, own_grad) - r_delta[h, row, :])
                dscore = dscore + col * (nn(of_head(scaled, h), valt) - b_delta[j, h])
                dscore = dscore.astype(bf16)
                f_adds.append((a, rows, nn(m_keyt[j, rows], dscore), nn(m_gradt[j, rows], col.astype(bf16))))
                keys.append(own)
                grads.append(own_grad)
                dscores.append(dscore)
                attns.append(attn.astype(bf16))
            rm = nn(jnp.concatenate(dscores, axis=1), jnp.concatenate(keys, axis=0))
            vm = nn(jnp.concatenate(attns, axis=1), jnp.concatenate(grads, axis=0))
            m_adds.append((j, rm, vm))
        for a, rows, rf, vf in f_adds:
            d_rf[a, rows] += rf
            d_vf[a, rows] += vf
        for j, rm, vm in m_adds:
            d_rm[j] += rm
            d_vm[j] += vm
        return 0

    lax.fori_loop(0, todo[NA * NZ + 8], visit, 0)
    for a in range(NA):
        for h in range(HEADS):
            rows = slice(h * DH, (h + 1) * DH)
            out_num[a, rows] = f_num[a, rows] * r_own[h * NA + a : h * NA + a + 1]
    for i in range(NG):
        s, k = i % NX, i // NX
        f = lax.rem(at[0] + s, NX) * NC + lax.rem(at[2] + k, NC)
        to = f_send if k else f_keep[s]
        for b in range(FB):
            base = (k * s * FB + b) * 3 * BLK
            to[base : base + BLK] = out_num[f * FB + b].astype(bf16)
            to[base + BLK : base + 2 * BLK] = d_rf[f * FB + b].astype(bf16)
            to[base + 2 * BLK : base + 3 * BLK] = d_vf[f * FB + b].astype(bf16)
    for j in range(NZ):
        b_max[j, 0] = m_num[j] * both_heads(3 * nc + j)
    for i in range(NZ):
        s, k = i % NP, i // NP
        near = at[1] + k * (1 - 2 * lax.rem(at[1], 2))
        j = lax.rem(near + 2 * s, NZ)
        to, base = (m_send, s * M_ROWS) if k else (m_keep[s], 0)
        to[base : base + BLK] = b_max[j, 0].astype(bf16)
        to[base + BLK : base + 2 * BLK] = d_rm[j].astype(bf16)
        to[base + 2 * BLK : base + 3 * BLK] = d_vm[j].astype(bf16)


def finish_kernel(at, *refs):
    x, weights, refs = refs[:NM], refs[NM : NM + 4], refs[NM + 4 :]
    f_parts, m_parts, refs = refs[: NX + 1], refs[NX + 1 : NX + NP + 2], refs[NX + NP + 2 :]
    fluid_out, metal_out, keep, send, dx = refs[0], refs[1], refs[2], refs[3], refs[4:]
    w_rf, w_vf, w_rm, w_vm = weights
    f_sum = functools.reduce(jnp.add, [p[0 : 3 * FB * BLK].astype(f32) for p in f_parts])
    m_sum = functools.reduce(jnp.add, [p[0:M_ROWS].astype(f32) for p in m_parts])
    rf, vf = [], []
    for i in range(FB):
        base = i * 3 * BLK
        fluid_out[i * BLK : (i + 1) * BLK] = f_sum[base : base + BLK].T.astype(bf16)
        rf.append(f_sum[base + BLK : base + 2 * BLK].T.astype(bf16))
        vf.append(f_sum[base + 2 * BLK : base + 3 * BLK].T.astype(bf16))
    rf, vf = jnp.concatenate(rf, axis=0), jnp.concatenate(vf, axis=0)
    metal_out[...] = m_sum[0:BLK].astype(bf16)
    rm, vm = m_sum[BLK : 2 * BLK].astype(bf16), m_sum[2 * BLK :].astype(bf16)
    split = FB * BLK
    for i in range(NM):
        rows = pl.ds(pl.multiple_of(lax.rem(at[3] + i, NM) * BLK, BLK), BLK)
        dx[i][0:split] = (nt(rf, w_rf[rows, :]) + nt(vf, w_vf[rows, :])).astype(bf16)
        dx[i][split:] = (nt(rm, w_rm[rows, :]) + nt(vm, w_vm[rows, :])).astype(bf16)
        fluid, metal = x[i][0:split], x[i][split:]
        start = lax.rem(at[3] - i + NM, NM) * BLK
        grads = [tn(fluid, rf), tn(fluid, vf), tn(metal, rm), tn(metal, vm)]
        for k in range(2):
            rows = pl.ds(pl.multiple_of(k * NM * BLK + start, BLK), BLK)
            keep[rows, :] = jnp.where(at[2] == 0, grads[k], grads[k + 2])
            send[rows, :] = jnp.where(at[2] == 0, grads[k + 2], grads[k])


def half_kernel(*refs):
    n = len(refs) // 2
    kept, came, out = refs[:n], refs[n], refs[n + 1 :]
    for s in range(n):
        rows = kept[s].shape[0]
        out[s][...] = (kept[s][...].astype(f32) + came[(s + 1) * rows : (s + 2) * rows].astype(f32)).astype(bf16)


def quarter_kernel(at, keep, came, own, *out):
    for s in range(NX):
        start = pl.multiple_of(lax.rem(at[0] + s, NX) * WROWS, WROWS)
        both = keep[pl.ds(start, WROWS), :] + came[pl.ds(start, WROWS), :]
        if s:
            out[s - 1][...] = both.astype(bf16)
        else:
            own[...] = both


def sum_kernel(*refs):
    refs[-1][...] = functools.reduce(jnp.add, [p[...].astype(f32) for p in refs[:-1]]).astype(bf16)


def total_kernel(at, *refs):
    parts, out, place = refs[:NP], refs[NP], refs[NP + 1]
    for s in range(NP):
        place[lax.rem(lax.div(at[1], 2) - s + NP, NP)] = parts[s][...]
    out[...] = functools.reduce(jnp.add, [place[s].astype(f32) for s in range(NP)])


def last_kernel(at, *refs):
    near, far, parts, (fluid, metal, wg) = refs[:NX], refs[NX : 2 * NX], refs[2 * NX : 2 * NX + NM], refs[2 * NX + NM :]
    total = functools.reduce(jnp.add, [p[...].astype(f32) for p in parts]).astype(bf16)
    fluid[...] = total[: FB * BLK]
    metal[...] = total[FB * BLK :]
    for s in range(NX):
        place = lax.rem(at[0] - s + NX, NX)
        for c, piece in ((at[2], near[s]), (1 - at[2], far[s])):
            wg[pl.ds(pl.multiple_of((c * NX + place) * WROWS, WROWS), WROWS), :] = piece[...]


def pack_kernel(fluid, metal, out):
    out[0 : FB * BLK] = fluid[...]
    out[FB * BLK :] = metal[...]


def call(kernel, out, args, scalars, scratch=(), smem_outs=()):
    return pl.pallas_call(
        kernel,
        out_shape=[jax.ShapeDtypeStruct(*o) for o in out],
        in_specs=[SMEM] * scalars + [VMEM] * (len(args) - scalars),
        out_specs=[SMEM if i in smem_outs else VMEM for i in range(len(out))],
        scratch_shapes=scratch,
        compiler_params=PARAMS,
    )(*args)


def shift(value, axis, n, s):
    return lax.ppermute(value, axis, [(i, (i + s) % n) for i in range(n)])


def pieces(value, axis, n):
    return [value] + [shift(value, axis, n, s) for s in range(1, n)]


def group_pieces(value):
    near = pieces(value, "x", NX)
    return near + [shift(p, "c", NC, 1) for p in near]


def across(value, axis, n, step):
    return lax.ppermute(value, axis, [(i, i ^ step) for i in range(n)])


def doubled(value, axis, n):
    value, step = value[None], n // 2
    while step:
        value, step = jnp.concatenate([value, across(value, axis, n, step)], axis=0), step // 2
    return value


def halves(kept, came, axis, n, step):
    sums = call(half_kernel, [(p.shape, bf16) for p in kept[1:]], [*kept[1:], came], 0)
    parts = [kept[0], came]
    for s, both in enumerate(sums, 1):
        parts.append(shift(both, axis, n, s * step))
    return parts


def body(fluid_x, metal_x, w_rf, w_vf, w_rm, w_vm, fluid_grad, metal_grad, pair_list, pair_count):
    weights = [w_rf, w_vf, w_rm, w_vm]
    at = jnp.stack([lax.axis_index(k) for k in ("x", "z", "c", "m")]).astype(jnp.int32)
    (x,) = call(pack_kernel, [(((FB + 1) * BLK, BLK), bf16)], [fluid_x, metal_x], 0)
    x = pieces(x, "m", NM)
    f_pay, m_pay = call(
        project_kernel,
        [((F_ROWS, BLK), bf16), ((M_ROWS, BLK), bf16)],
        [at, pair_count, *x, *weights, fluid_grad, metal_grad, pair_list],
        2,
    )
    f_in = lax.all_gather(f_pay, XC, axis=0)
    m_in = pieces(m_pay, "z", NZ)
    table = f_in[:, 3 * FB * BLK].reshape(NA, NX, NZ, NC)
    table = lax.dynamic_index_in_dim(table, at[0], 1, False)
    table = lax.dynamic_index_in_dim(table, at[2], 2, False)
    live = (table.reshape(NA * NZ) > 0).astype(jnp.int32)
    block = (BLK, BLK)
    moved = pltpu.VMEM((NZ + 1, M_ROWS, BLK), bf16)
    f_acc, m_acc = pltpu.VMEM((NA + 1, *block), f32), pltpu.VMEM((NZ + 1, *block), f32)
    m_tiles = pltpu.VMEM((NZ + 1, *block), bf16)
    r_rows = pltpu.VMEM((HEADS, NA + 8, BLK), f32)
    tiles = pltpu.VMEM((NZ + 1, HEADS, *block), f32)
    r_own, c_own, f_num, m_num, todo = call(
        forward_kernel,
        [
            ((3 * HEADS * NA, BLK), f32),
            ((3 * HEADS * NZ, BLK), f32),
            ((NA, *block), f32),
            ((NZ, *block), f32),
            ((NA * NZ + 16,), jnp.int32),
        ],
        [at, live, f_in, *m_in],
        2,
        [moved, m_tiles, f_acc, m_acc, r_rows, r_rows, tiles, tiles],
        smem_outs=(4,),
    )
    c_in = doubled(c_own, "z", NZ)
    r_in = group_pieces(r_own)
    out = call(
        backward_kernel,
        [((3 * FB * BLK, BLK), bf16)] * NX
        + [((NX * 3 * FB * BLK, BLK), bf16)]
        + [((M_ROWS, BLK), bf16)] * NP
        + [((NP * M_ROWS, BLK), bf16)],
        [at, todo, f_in, *m_in, *r_in, c_in, f_num, m_num],
        2,
        [moved, m_tiles, m_tiles, m_tiles, tiles, tiles, r_rows, r_rows, r_rows, f_acc, f_acc, m_acc, m_acc, f_acc],
    )
    f_part = halves(out[:NX], shift(out[NX], "c", NC, 1), "x", NX, 1)
    m_part = halves(out[NX + 1 : -1], across(out[-1], "z", NZ, 1), "z", NZ, 2)
    fluid_out, metal_out, keep, send, *dx = call(
        finish_kernel,
        [
            ((FB * BLK, BLK), bf16),
            ((BLK, BLK), bf16),
            ((NX * WROWS, BLK), f32),
            ((NX * WROWS, BLK), f32),
        ]
        + [(((FB + 1) * BLK, BLK), bf16)] * NM,
        [at, *x, *weights, *f_part, *m_part],
        1,
    )
    dx = [dx[0]] + [shift(dx[s], "m", NM, s) for s in range(1, NM)]
    came = shift(send, "c", NC, 1)
    piece = (WROWS, BLK)
    own, *parts = call(quarter_kernel, [(piece, f32)] + [(piece, bf16)] * (NX - 1), [at, keep, came], 1)
    parts = [shift(p, "x", NX, s) for s, p in enumerate(parts, 1)]
    (wg,) = call(sum_kernel, [(piece, bf16)], [own, *parts], 0)
    came, dx = lax.optimization_barrier((across(wg, "z", NZ, 1), dx))
    (wg,) = call(sum_kernel, [(piece, bf16)], [wg, came], 0)
    (wg,) = call(
        total_kernel,
        [(piece, f32)],
        [at, wg] + [shift(wg, "z", NZ, 2 * s) for s in range(1, NP)],
        1,
        [pltpu.VMEM((NP, *piece), bf16)],
    )
    near = pieces(wg, "x", NX)
    far = [shift(p, "c", NC, 1) for p in near]
    fluid_dx, metal_dx, wg = call(
        last_kernel,
        [((FB * BLK, BLK), bf16), ((BLK, BLK), bf16), ((NG * WROWS, BLK), f32)],
        [at, *near, *far, *dx],
        1,
    )
    return fluid_out, metal_out, fluid_dx, metal_dx, wg.reshape(4, NM * BLK, BLK)


def solution(mesh):
    grid = Mesh(mesh.devices.reshape(NX, NZ, NC, NM), ("x", "z", "c", "m"))
    tokens, weight = P(FLUID, "m"), P(None, "m")
    return jax.shard_map(
        body,
        mesh=grid,
        in_specs=(tokens, tokens, weight, weight, weight, weight, tokens, tokens, P(FLUID, None), P(FLUID)),
        out_specs=(tokens, tokens, tokens, tokens, P(None, None, "m")),
        check_vma=False,
    )
```

```python
import functools

import jax
import jax.numpy as jnp
from jax import lax
from jax.experimental import pallas as pl
from jax.experimental.pallas import tpu as pltpu
from jax.sharding import Mesh, PartitionSpec as P

BLK = 128
HEADS = 2
DH = 64
NX, NZ, NC, NM = 4, 8, 2, 4
NG = NX * NC
FB = 2
NP = NZ // 2
WROWS = 4 * NM * BLK // NG
NA = NG * FB
LOWEST = -1e30
ROOT = 0.125
XC = ("x", "c")
FLUID = ("x", "z", "c")
F_ROWS = 3 * FB * BLK + 16
M_ROWS = 3 * BLK
f32, bf16 = jnp.float32, jnp.bfloat16
PARAMS = pltpu.CompilerParams(vmem_limit_bytes=24 * 2**20)
VMEM = pl.BlockSpec(memory_space=pltpu.VMEM)
SMEM = pl.BlockSpec(memory_space=pltpu.SMEM)
AT_ONCE = 4
CELL = 16


def nn(a, b):
    return lax.dot_general(a, b, (((1,), (0,)), ((), ())), preferred_element_type=f32)


def nt(a, b):
    return lax.dot_general(a, b, (((1,), (1,)), ((), ())), preferred_element_type=f32)


def tn(a, b):
    return lax.dot_general(a, b, (((0,), (0,)), ((), ())), preferred_element_type=f32)


def head_mask(h):
    lane = lax.broadcasted_iota(jnp.int32, (BLK, BLK), 1)
    return lane < DH if h == 0 else lane >= DH


def of_head(tile, h):
    return jnp.where(head_mask(h), tile, jnp.zeros_like(tile))


def project_kernel(at, count, *refs):
    x, w, refs = refs[:NM], refs[NM : NM + 4], refs[NM + 4 :]
    f_grad, m_grad, pairs, f_pay, m_pay = refs
    f_pay[2 * FB * BLK : 3 * FB * BLK] = f_grad[...]
    m_pay[2 * BLK :] = m_grad[...]
    m = at[3]
    slots = pairs.shape[0]
    code = pairs[:, 0:1] * (NX * NZ * NC) + pairs[:, 1:2]
    lane = lax.broadcasted_iota(jnp.int32, (slots, BLK), 1)
    slot = lax.broadcasted_iota(jnp.int32, (slots, BLK), 0)
    hit = jnp.where((code == lane) & (slot < count[0]), 1.0, 0.0)
    table = jnp.max(hit, axis=0, keepdims=True)
    f_pay[3 * FB * BLK :] = jnp.broadcast_to(table, (16, BLK)).astype(bf16)

    def project(rows, k):
        total = None
        for s in range(NM):
            start = pl.multiple_of(lax.rem(m - s + NM, NM) * BLK, BLK)
            part = nn(x[s][rows], w[k][pl.ds(start, BLK), :])
            total = part if total is None else total + part
        return total

    fluid, metal = slice(0, FB * BLK), slice(FB * BLK, FB * BLK + BLK)
    f_pay[0 : FB * BLK] = project(fluid, 0).astype(bf16)
    values = project(fluid, 1).astype(bf16)
    for i in range(FB):
        start = (FB + i) * BLK
        f_pay[start : start + BLK] = values[i * BLK : (i + 1) * BLK].T
    m_pay[0:BLK] = project(metal, 2).astype(bf16)
    m_pay[BLK : 2 * BLK] = project(metal, 3).astype(bf16)


def bring(at, m_in, m_all):
    for s in range(NZ):
        m_all[lax.rem(at[1] - s + NZ, NZ)] = m_in[s][...]


def f_tile(f_all, a, part):
    start = pl.multiple_of(part * FB * BLK + lax.rem(a, FB) * BLK, BLK)
    return f_all[jnp.minimum(lax.div(a, FB), NG - 1), pl.ds(start, BLK), :]


def spread(tile, k):
    return jnp.broadcast_to(tile[:, k : k + 1], (BLK, BLK))


def pair_at(todo, i):
    cell = todo[i]
    return lax.div(cell, CELL), lax.rem(cell, CELL)


def forward_kernel(at, live, f_all, *refs):
    m_in, refs = refs[:NZ], refs[NZ:]
    r_stat, c_stat, f_num, m_num, todo = refs[:5]
    m_all, m_valt, f_acc, m_acc, r_max, r_sum, c_top, c_sum = refs[5:]
    bring(at, m_in, m_all)

    def list_step(a, n):
        for j in range(NZ):
            todo[n] = a * CELL + j
            n = n + live[a * NZ + j]
        return n

    total = lax.fori_loop(0, NA, list_step, 0)
    for k in range(AT_ONCE):
        todo[total + k] = NA * CELL + NZ
    turns = lax.div(total + AT_ONCE - 1, AT_ONCE)
    todo[NA * NZ + 8] = turns
    for ref in (r_max, c_top):
        ref[...] = jnp.full(ref.shape, LOWEST, f32)
    for ref in (r_sum, c_sum, f_acc, m_acc):
        ref[...] = jnp.zeros_like(ref)

    def scores_of(a, j):
        key = f_tile(f_all, a, 0) * jnp.asarray(ROOT, bf16)
        return [nt(m_all[j, 0:BLK], of_head(key, h)) for h in range(HEADS)]

    def max_step(i, _):
        tops = []
        for k in range(AT_ONCE):
            a, j = pair_at(todo, i * AT_ONCE + k)
            for h, scores in enumerate(scores_of(a, j)):
                tops.append((h, a, j, scores, jnp.max(scores, axis=0, keepdims=True)))
        for h, a, j, scores, top in tops:
            r_max[h, pl.ds(a, 1), :] = jnp.maximum(r_max[h, pl.ds(a, 1), :], top)
            c_top[j, h] = jnp.maximum(c_top[j, h], scores)
        return 0

    lax.fori_loop(0, turns, max_step, 0)
    lane = lax.broadcasted_iota(jnp.int32, (BLK, BLK), 1)
    down = jnp.zeros((BLK, BLK), f32)
    for j in range(NZ):
        m_valt[j] = m_all[j, BLK : 2 * BLK].T
        for h in range(HEADS):
            top = jnp.broadcast_to(jnp.max(c_top[j, h], axis=1, keepdims=True), (BLK, BLK))
            c_top[j, h] = top
            down = jnp.where(lane == h * NZ + j, top, down)

    def sum_step(i, _):
        f_adds, m_adds = [], []
        for k in range(AT_ONCE):
            a, j = pair_at(todo, i * AT_ONCE + k)
            valt, othert = f_tile(f_all, a, 1), m_valt[j]
            parts = []
            for h, scores in enumerate(scores_of(a, j)):
                rows = slice(h * DH, (h + 1) * DH)
                part = jnp.exp(scores - r_max[h, pl.ds(a, 1), :])
                f_adds.append((h, a, jnp.sum(part, axis=0, keepdims=True), nn(othert[rows], part.astype(bf16))))
                parts.append(jnp.exp(scores - c_top[j, h]))
            left = jnp.concatenate([p.astype(bf16) for p in parts], axis=1)
            zero = jnp.zeros((DH, BLK), bf16)
            right = jnp.concatenate(
                [jnp.concatenate([valt[:DH], zero], axis=0), jnp.concatenate([zero, valt[DH:]], axis=0)], axis=1
            )
            m_adds.append((j, parts, nt(left, right)))
        for h, a, total, num in f_adds:
            r_sum[h, pl.ds(a, 1), :] += total
            f_acc[a, h * DH : (h + 1) * DH] += num
        for j, parts, num in m_adds:
            for h in range(HEADS):
                c_sum[j, h] += parts[h]
            m_acc[j] += num
        return 0

    lax.fori_loop(0, turns, sum_step, 0)
    for h in range(HEADS):
        for k, ref in enumerate((r_max, r_sum)):
            r_stat[(k * HEADS + h) * NA : (k * HEADS + h + 1) * NA] = ref[h, 0:NA]
    f_num[...] = f_acc[0:NA]
    m_num[...] = m_acc[0:NZ]
    for a in range(NA):
        start = (2 * FB + a % FB) * BLK
        gradt = f_all[a // FB, start : start + BLK, :].T
        for h in range(HEADS):
            rows = slice(h * DH, (h + 1) * DH)
            row = (2 * HEADS + h) * NA + a
            r_stat[row : row + 1] = jnp.sum(gradt[rows].astype(f32) * f_acc[a, rows], axis=0, keepdims=True)
    nc = HEADS * NZ
    for j in range(NZ):
        product = m_all[j, 2 * BLK : 3 * BLK].astype(f32) * m_acc[j]
        for h in range(HEADS):
            k = h * NZ + j
            down = jnp.where(lane == nc + k, jnp.sum(c_sum[j, h], axis=1, keepdims=True), down)
            down = jnp.where(lane == 2 * nc + k, jnp.sum(of_head(product, h), axis=1, keepdims=True), down)
    across = down.T[0 : 3 * nc]
    c_stat[...] = across


def merge(parts, own, n):
    top = functools.reduce(jnp.maximum, [p[0:n] for p in parts])
    fades = [jnp.exp(p[0:n] - top) for p in parts]
    total = functools.reduce(jnp.add, [w * p[n : 2 * n] for w, p in zip(fades, parts)])
    delta = functools.reduce(jnp.add, [w * p[2 * n : 3 * n] for w, p in zip(fades, parts)])
    safe = jnp.where(total > 0, total, 1.0)
    return top, safe, delta / safe, jnp.exp(own[0:n] - top) / safe


def backward_kernel(at, todo, f_all, *refs):
    m_in, refs = refs[:NZ], refs[NZ:]
    r_in, c_in, f_num, m_num, refs = refs[:NG], refs[NG], refs[NG + 1], refs[NG + 2], refs[NG + 3 :]
    f_keep, f_send, refs = refs[:NX], refs[NX], refs[NX + 1 :]
    m_keep, m_send, refs = refs[:NP], refs[NP], refs[NP + 1 :]
    m_all, m_keyt, m_grad, m_gradt, b_max, b_delta, r_max, r_inv, r_delta, d_rf, d_vf, d_rm, d_vm, out_num = refs
    bring(at, m_in, m_all)
    nr, nc = HEADS * NA, HEADS * NZ
    for ref in (d_rf, d_vf, d_rm, d_vm):
        ref[...] = jnp.zeros_like(ref)
    top, total, delta, r_own = merge(r_in, r_in[0], nr)
    inv = 1.0 / total
    for h in range(HEADS):
        rows = slice(h * NA, (h + 1) * NA)
        r_max[h, 0:NA] = top[rows]
        r_inv[h, 0:NA] = inv[rows]
        r_delta[h, 0:NA] = delta[rows]
    top, total, delta, c_fade = merge([c_in.at[p] for p in range(NZ)], c_in.at[0], nc)
    delta = delta / total
    pad = jnp.zeros((BLK - 4 * nc, BLK), f32)
    down = jnp.concatenate([top, total, delta, c_fade, pad], axis=0).T

    def both_heads(k):
        return jnp.where(head_mask(0), spread(down, k), spread(down, k + NZ))

    for j in range(NZ):
        for h in range(HEADS):
            b_max[j, h] = spread(down, h * NZ + j)
            b_delta[j, h] = spread(down, 2 * nc + h * NZ + j)
        m_keyt[j] = (m_all[j, 0:BLK] * jnp.asarray(ROOT, bf16)).T
        scaled = (m_all[j, 2 * BLK : 3 * BLK].astype(f32) / both_heads(nc + j)).astype(bf16)
        m_grad[j] = scaled
        m_gradt[j] = scaled.T

    def visit(i, _):
        f_adds, m_adds = [], []
        for n in range(AT_ONCE):
            a, j = pair_at(todo, i * AT_ONCE + n)
            row = pl.ds(a, 1)
            key = f_tile(f_all, a, 0) * jnp.asarray(ROOT, bf16)
            valt = f_tile(f_all, a, 1)
            grad = f_tile(f_all, a, 2)
            other, other_val, scaled = m_all[j, 0:BLK], m_all[j, BLK : 2 * BLK], m_grad[j]
            keys, grads, dscores, attns = [], [], [], []
            for h in range(HEADS):
                rows = slice(h * DH, (h + 1) * DH)
                own, own_grad = of_head(key, h), of_head(grad, h)
                scores = nt(other, own)
                attn = jnp.exp(scores - r_max[h, row, :]) * r_inv[h, row, :]
                col = jnp.exp(scores - b_max[j, h])
                dscore = attn * (nt(other_val, own_grad) - r_delta[h, row, :])
                dscore = dscore + col * (nn(of_head(scaled, h), valt) - b_delta[j, h])
                dscore = dscore.astype(bf16)
                f_adds.append((a, rows, nn(m_keyt[j, rows], dscore), nn(m_gradt[j, rows], col.astype(bf16))))
                keys.append(own)
                grads.append(own_grad)
                dscores.append(dscore)
                attns.append(attn.astype(bf16))
            rm = nn(jnp.concatenate(dscores, axis=1), jnp.concatenate(keys, axis=0))
            vm = nn(jnp.concatenate(attns, axis=1), jnp.concatenate(grads, axis=0))
            m_adds.append((j, rm, vm))
        for a, rows, rf, vf in f_adds:
            d_rf[a, rows] += rf
            d_vf[a, rows] += vf
        for j, rm, vm in m_adds:
            d_rm[j] += rm
            d_vm[j] += vm
        return 0

    lax.fori_loop(0, todo[NA * NZ + 8], visit, 0)
    for a in range(NA):
        for h in range(HEADS):
            rows = slice(h * DH, (h + 1) * DH)
            out_num[a, rows] = f_num[a, rows] * r_own[h * NA + a : h * NA + a + 1]
    for i in range(NG):
        s, k = i % NX, i // NX
        f = lax.rem(at[0] + s, NX) * NC + lax.rem(at[2] + k, NC)
        to = f_send if k else f_keep[s]
        for b in range(FB):
            base = (k * s * FB + b) * 3 * BLK
            to[base : base + BLK] = out_num[f * FB + b].astype(bf16)
            to[base + BLK : base + 2 * BLK] = d_rf[f * FB + b].astype(bf16)
            to[base + 2 * BLK : base + 3 * BLK] = d_vf[f * FB + b].astype(bf16)
    for j in range(NZ):
        b_max[j, 0] = m_num[j] * both_heads(3 * nc + j)
    for i in range(NZ):
        s, k = i % NP, i // NP
        near = at[1] + k * (1 - 2 * lax.rem(at[1], 2))
        j = lax.rem(near + 2 * s, NZ)
        to, base = (m_send, s * M_ROWS) if k else (m_keep[s], 0)
        to[base : base + BLK] = b_max[j, 0].astype(bf16)
        to[base + BLK : base + 2 * BLK] = d_rm[j].astype(bf16)
        to[base + 2 * BLK : base + 3 * BLK] = d_vm[j].astype(bf16)


def finish_kernel(at, *refs):
    x, weights, refs = refs[:NM], refs[NM : NM + 4], refs[NM + 4 :]
    f_parts, m_parts, refs = refs[: NX + 1], refs[NX + 1 : NX + NP + 2], refs[NX + NP + 2 :]
    fluid_out, metal_out, keep, send, dx = refs[0], refs[1], refs[2], refs[3], refs[4:]
    w_rf, w_vf, w_rm, w_vm = weights
    f_sum = functools.reduce(jnp.add, [p[0 : 3 * FB * BLK].astype(f32) for p in f_parts])
    m_sum = functools.reduce(jnp.add, [p[0:M_ROWS].astype(f32) for p in m_parts])
    rf, vf = [], []
    for i in range(FB):
        base = i * 3 * BLK
        fluid_out[i * BLK : (i + 1) * BLK] = f_sum[base : base + BLK].T.astype(bf16)
        rf.append(f_sum[base + BLK : base + 2 * BLK].T.astype(bf16))
        vf.append(f_sum[base + 2 * BLK : base + 3 * BLK].T.astype(bf16))
    rf, vf = jnp.concatenate(rf, axis=0), jnp.concatenate(vf, axis=0)
    metal_out[...] = m_sum[0:BLK].astype(bf16)
    rm, vm = m_sum[BLK : 2 * BLK].astype(bf16), m_sum[2 * BLK :].astype(bf16)
    split = FB * BLK
    for i in range(NM):
        rows = pl.ds(pl.multiple_of(lax.rem(at[3] + i, NM) * BLK, BLK), BLK)
        dx[i][0:split] = (nt(rf, w_rf[rows, :]) + nt(vf, w_vf[rows, :])).astype(bf16)
        dx[i][split:] = (nt(rm, w_rm[rows, :]) + nt(vm, w_vm[rows, :])).astype(bf16)
        fluid, metal = x[i][0:split], x[i][split:]
        start = lax.rem(at[3] - i + NM, NM) * BLK
        grads = [tn(fluid, rf), tn(fluid, vf), tn(metal, rm), tn(metal, vm)]
        for k in range(2):
            rows = pl.ds(pl.multiple_of(k * NM * BLK + start, BLK), BLK)
            keep[rows, :] = jnp.where(at[2] == 0, grads[k], grads[k + 2])
            send[rows, :] = jnp.where(at[2] == 0, grads[k + 2], grads[k])


def half_kernel(*refs):
    n = len(refs) // 2
    kept, came, out = refs[:n], refs[n], refs[n + 1 :]
    for s in range(n):
        rows = kept[s].shape[0]
        out[s][...] = (kept[s][...].astype(f32) + came[(s + 1) * rows : (s + 2) * rows].astype(f32)).astype(bf16)


def quarter_kernel(at, keep, came, own, *out):
    for s in range(NX):
        start = pl.multiple_of(lax.rem(at[0] + s, NX) * WROWS, WROWS)
        both = keep[pl.ds(start, WROWS), :] + came[pl.ds(start, WROWS), :]
        if s:
            out[s - 1][...] = both.astype(bf16)
        else:
            own[...] = both


def sum_kernel(*refs):
    refs[-1][...] = functools.reduce(jnp.add, [p[...].astype(f32) for p in refs[:-1]]).astype(bf16)


def total_kernel(at, *refs):
    parts, out, place = refs[:NP], refs[NP], refs[NP + 1]
    for s in range(NP):
        place[lax.rem(lax.div(at[1], 2) - s + NP, NP)] = parts[s][...]
    out[...] = functools.reduce(jnp.add, [place[s].astype(f32) for s in range(NP)])


def last_kernel(at, *refs):
    near, far, parts, (fluid, metal, wg) = refs[:NX], refs[NX : 2 * NX], refs[2 * NX : 2 * NX + NM], refs[2 * NX + NM :]
    total = functools.reduce(jnp.add, [p[...].astype(f32) for p in parts]).astype(bf16)
    fluid[...] = total[: FB * BLK]
    metal[...] = total[FB * BLK :]
    for s in range(NX):
        place = lax.rem(at[0] - s + NX, NX)
        for c, piece in ((at[2], near[s]), (1 - at[2], far[s])):
            wg[pl.ds(pl.multiple_of((c * NX + place) * WROWS, WROWS), WROWS), :] = piece[...]


def pack_kernel(fluid, metal, out):
    out[0 : FB * BLK] = fluid[...]
    out[FB * BLK :] = metal[...]


def call(kernel, out, args, scalars, scratch=(), smem_outs=()):
    return pl.pallas_call(
        kernel,
        out_shape=[jax.ShapeDtypeStruct(*o) for o in out],
        in_specs=[SMEM] * scalars + [VMEM] * (len(args) - scalars),
        out_specs=[SMEM if i in smem_outs else VMEM for i in range(len(out))],
        scratch_shapes=scratch,
        compiler_params=PARAMS,
    )(*args)


def shift(value, axis, n, s):
    return lax.ppermute(value, axis, [(i, (i + s) % n) for i in range(n)])


def pieces(value, axis, n):
    return [value] + [shift(value, axis, n, s) for s in range(1, n)]


def across(value, axis, n, step):
    return lax.ppermute(value, axis, [(i, i ^ step) for i in range(n)])


def joined(value, axis, n, step):
    return jnp.concatenate([value, across(value, axis, n, step)], axis=0)


def halves(kept, came, axis, n, step):
    sums = call(half_kernel, [(p.shape, bf16) for p in kept[1:]], [*kept[1:], came], 0)
    parts = [kept[0], came]
    for s, both in enumerate(sums, 1):
        parts.append(shift(both, axis, n, s * step))
    return parts


def body(fluid_x, metal_x, w_rf, w_vf, w_rm, w_vm, fluid_grad, metal_grad, pair_list, pair_count):
    weights = [w_rf, w_vf, w_rm, w_vm]
    at = jnp.stack([lax.axis_index(k) for k in ("x", "z", "c", "m")]).astype(jnp.int32)
    (x,) = call(pack_kernel, [(((FB + 1) * BLK, BLK), bf16)], [fluid_x, metal_x], 0)
    x = pieces(x, "m", NM)
    f_pay, m_pay = call(
        project_kernel,
        [((F_ROWS, BLK), bf16), ((M_ROWS, BLK), bf16)],
        [at, pair_count, *x, *weights, fluid_grad, metal_grad, pair_list],
        2,
    )
    f_in = lax.all_gather(f_pay, XC, axis=0)
    m_in = pieces(m_pay, "z", NZ)
    table = f_in[:, 3 * FB * BLK].reshape(NA, NX, NZ, NC)
    table = lax.dynamic_index_in_dim(table, at[0], 1, False)
    table = lax.dynamic_index_in_dim(table, at[2], 2, False)
    live = (table.reshape(NA * NZ) > 0).astype(jnp.int32)
    block = (BLK, BLK)
    moved = pltpu.VMEM((NZ + 1, M_ROWS, BLK), bf16)
    f_acc, m_acc = pltpu.VMEM((NA + 1, *block), f32), pltpu.VMEM((NZ + 1, *block), f32)
    m_tiles = pltpu.VMEM((NZ + 1, *block), bf16)
    r_rows = pltpu.VMEM((HEADS, NA + 8, BLK), f32)
    tiles = pltpu.VMEM((NZ + 1, HEADS, *block), f32)
    r_own, c_own, f_num, m_num, todo = call(
        forward_kernel,
        [
            ((3 * HEADS * NA, BLK), f32),
            ((3 * HEADS * NZ, BLK), f32),
            ((NA, *block), f32),
            ((NZ, *block), f32),
            ((NA * NZ + 16,), jnp.int32),
        ],
        [at, live, f_in, *m_in],
        2,
        [moved, m_tiles, f_acc, m_acc, r_rows, r_rows, tiles, tiles],
        smem_outs=(4,),
    )
    near, c_in = lax.optimization_barrier((pieces(r_own, "x", NX), joined(c_own[None], "z", NZ, 4)))
    r_in = near + [shift(p, "c", NC, 1) for p in near]
    c_in = joined(joined(c_in, "z", NZ, 2), "z", NZ, 1)
    out = call(
        backward_kernel,
        [((3 * FB * BLK, BLK), bf16)] * NX
        + [((NX * 3 * FB * BLK, BLK), bf16)]
        + [((M_ROWS, BLK), bf16)] * NP
        + [((NP * M_ROWS, BLK), bf16)],
        [at, todo, f_in, *m_in, *r_in, c_in, f_num, m_num],
        2,
        [moved, m_tiles, m_tiles, m_tiles, tiles, tiles, r_rows, r_rows, r_rows, f_acc, f_acc, m_acc, m_acc, f_acc],
    )
    f_part = halves(out[:NX], shift(out[NX], "c", NC, 1), "x", NX, 1)
    m_part = halves(out[NX + 1 : -1], across(out[-1], "z", NZ, 1), "z", NZ, 2)
    fluid_out, metal_out, keep, send, *dx = call(
        finish_kernel,
        [
            ((FB * BLK, BLK), bf16),
            ((BLK, BLK), bf16),
            ((NX * WROWS, BLK), f32),
            ((NX * WROWS, BLK), f32),
        ]
        + [(((FB + 1) * BLK, BLK), bf16)] * NM,
        [at, *x, *weights, *f_part, *m_part],
        1,
    )
    dx = [dx[0]] + [shift(dx[s], "m", NM, s) for s in range(1, NM)]
    came = shift(send, "c", NC, 1)
    piece = (WROWS, BLK)
    own, *parts = call(quarter_kernel, [(piece, f32)] + [(piece, bf16)] * (NX - 1), [at, keep, came], 1)
    parts = [shift(p, "x", NX, s) for s, p in enumerate(parts, 1)]
    (wg,) = call(sum_kernel, [(piece, bf16)], [own, *parts], 0)
    came, dx = lax.optimization_barrier((across(wg, "z", NZ, 1), dx))
    (wg,) = call(sum_kernel, [(piece, bf16)], [wg, came], 0)
    (wg,) = call(
        total_kernel,
        [(piece, f32)],
        [at, wg] + [shift(wg, "z", NZ, 2 * s) for s in range(1, NP)],
        1,
        [pltpu.VMEM((NP, *piece), bf16)],
    )
    near = pieces(wg, "x", NX)
    far = [shift(p, "c", NC, 1) for p in near]
    fluid_dx, metal_dx, wg = call(
        last_kernel,
        [((FB * BLK, BLK), bf16), ((BLK, BLK), bf16), ((NG * WROWS, BLK), f32)],
        [at, *near, *far, *dx],
        1,
    )
    return fluid_out, metal_out, fluid_dx, metal_dx, wg.reshape(4, NM * BLK, BLK)


def solution(mesh):
    grid = Mesh(mesh.devices.reshape(NX, NZ, NC, NM), ("x", "z", "c", "m"))
    tokens, weight = P(FLUID, "m"), P(None, "m")
    return jax.shard_map(
        body,
        mesh=grid,
        in_specs=(tokens, tokens, weight, weight, weight, weight, tokens, tokens, P(FLUID, None), P(FLUID)),
        out_specs=(tokens, tokens, tokens, tokens, P(None, None, "m")),
        check_vma=False,
    )
```
